32 devices in a mesh: gx: 8 (over z, core), vert: 4 (over y, x).
Axes of the slice: x: 2, y: 2, z: 4, core: 2. Of those that a mesh axis runs over, the one named last changes fastest.
Arguments:
- distribution: float32 [4096, 8, 256], P('vert', 'gx'), may hold values from -6 to 6
- relax_rate: float32 [8, 256], P('gx'), may hold values from 0.3 to 3
- node_weight: float32 [4096], P('vert'), may hold values from 0.05 to 1
- kernel_tiles: bfloat16 [32, 128, 1536], P('vert'), may hold values from -0.15625 to 0.15625
- tile_cols: int32 [32, 12], P('vert'), may hold values from 0 to 31, as said below
Outputs:
- new_distribution: float32 [4096, 8, 256], P('vert', 'gx')
The draws below stay inside these ranges and needn't reach their ends.
Inputs may be any that keep to these rules, and one draw needn't show every extreme that they name: `tile_cols`: row block r lists its own block r first; the 12 column blocks listed for one row block are distinct.
All inputs are finite; a program needn't handle non-finite values.
Results may differ from the reference program's by a relative error of at most 0.0021.
Values may be sent and summed in bfloat16 or wider, within the bound.
A program may use at most 64 MiB of HBM per device.

```python
import math
import jax
import jax.numpy as jnp
from jax import lax

Q = 16
TILE = 128
NB = 12
NZ = 4
STEPS = 2
V = 4096
RBLK = 32
NYZ = 256
NX = 8


def draw_tile_cols(key, part):
    row_ids = jnp.arange(RBLK, dtype=jnp.int32)
    row_keys = jax.random.split(key, RBLK)
    others = jax.vmap(lambda row_key: jax.random.permutation(row_key, RBLK - 1))(row_keys)
    others = others[:, :NB - 1].astype(jnp.int32)
    others = others + (others >= row_ids[:, None]).astype(jnp.int32)
    return jnp.concatenate([row_ids[:, None], others], axis=1)


def block_scale(stream_key, dims, cuts, least, largest):
    def one(position, parts):
        heights = jax.random.uniform(jax.random.fold_in(jax.random.fold_in(stream_key, 6), position), (parts,), jnp.float32, least / len(cuts), largest / len(cuts))
        return jnp.repeat(jnp.exp(heights), dims[position] // parts).reshape((-1,) + (1,) * (len(dims) - position - 1))

    level = one(*cuts[0])
    for cut in cuts[1:]:
        level = level * one(*cut)
    return level


def gaussian(own_key, extent, deviation, limit, shards=(), kind=jnp.bfloat16):
    drawn = deviation * jax.random.normal(own_key, extent, jnp.float32)
    if shards:
        drawn = drawn * block_scale(own_key, extent, shards, -0.22, 0.18)
    return jnp.clip(drawn, -limit, limit).astype(kind)


def setup_inputs(seed: int = 0) -> dict:
    streams_of = jax.random.split(jax.random.key(seed), 6)
    return {
        "distribution": gaussian(streams_of[0], (V, NX, NYZ), 1.0, 6.0, ((0, 4), (1, 8)), jnp.float32),
        "relax_rate": jnp.clip(jnp.exp(math.log(3.0) - 2.3025851 * jax.random.uniform(streams_of[1], (NX, NYZ), jnp.float32) ** block_scale(streams_of[1], (NX, NYZ), ((0, 8),), -0.2, 0.2)), 0.3, 3.0),
        "node_weight": jnp.clip(jnp.exp(math.log(1.0) - 2.9957323 * jax.random.uniform(streams_of[2], (V,), jnp.float32) ** block_scale(streams_of[2], (V,), ((0, 4),), -0.2, 0.2)), 0.05, 1.0),
        "kernel_tiles": gaussian(streams_of[3], (RBLK, TILE, NB * TILE), (NB * TILE) ** -0.5, 0.15625, ((0, 4),)),
        "tile_cols": draw_tile_cols(jax.random.fold_in(streams_of[5], 71), 0),
    }


COURANT_SCALE = 0.3
KERNEL_STEP = 0.5
PRECISE = lax.Precision.HIGHEST

def node_components(first_node, node_count):
    node_index = first_node + jnp.arange(node_count, dtype=jnp.int32)
    middle = (Q - 1) / 2.0
    speed_x = ((node_index % Q).astype(jnp.float32) - middle) / middle
    speed_y = ((node_index // Q % Q).astype(jnp.float32) - middle) / middle
    speed_z = ((node_index // (Q * Q)).astype(jnp.float32) - middle) / middle
    courant = COURANT_SCALE * jnp.stack([speed_x, speed_y, speed_z])
    squares = speed_x * speed_x + speed_y * speed_y + speed_z * speed_z
    invariants = jnp.stack([jnp.ones_like(speed_x), speed_x, speed_y, speed_z, squares])
    return (courant, invariants)

def gram_inverse(weighted, invariants):
    gram_matrix = jnp.dot(weighted, invariants.T, precision=PRECISE)
    factor = jnp.linalg.cholesky(gram_matrix)
    return jax.scipy.linalg.cho_solve((factor, True), jnp.eye(5, dtype=gram_matrix.dtype))

def advect(source, lower_x, upper_x, courant):
    plane_size = source.shape[-1]
    z_index = jnp.arange(plane_size, dtype=jnp.int32) % NZ
    lower_y = jnp.roll(source, NZ, axis=-1)
    upper_y = jnp.roll(source, -NZ, axis=-1)
    lower_z = jnp.where(z_index == 0, jnp.roll(source, 1 - NZ, axis=-1), jnp.roll(source, 1, axis=-1))
    upper_z = jnp.where(z_index == NZ - 1, jnp.roll(source, NZ - 1, axis=-1), jnp.roll(source, -1, axis=-1))
    total_flux = jnp.zeros_like(source)
    for component, below, above in ((0, lower_x, upper_x), (1, lower_y, upper_y), (2, lower_z, upper_z)):
        node_speed = courant[component][:, None, None]
        total_flux = total_flux + jnp.maximum(node_speed, 0.0) * (source - below) + jnp.minimum(node_speed, 0.0) * (above - source)
    return source - total_flux

def reference(distribution, relax_rate, node_weight, kernel_tiles, tile_cols):
    courant, invariants = node_components(0, V)
    weighted = invariants * node_weight[None, :]
    inverse = gram_inverse(weighted, invariants)
    relax_share = relax_rate / (1.0 + relax_rate)
    speed_blocks = courant.reshape(3, RBLK, TILE).transpose(1, 0, 2)
    current = distribution
    for step_index in range(STEPS):
        rounded = current.astype(jnp.bfloat16)
        blocks = rounded.reshape(RBLK, TILE, -1)
        cell_count = blocks.shape[-1]

        def block_update(block_pair):
            tile_row, column_list, source, speeds = block_pair
            picked = jnp.take(blocks, column_list, axis=0).reshape(-1, cell_count)
            kernel_term = jnp.dot(tile_row.astype(jnp.float32), picked.astype(jnp.float32), preferred_element_type=jnp.float32).reshape(source.shape)
            advected = advect(source, jnp.roll(source, 1, axis=1), jnp.roll(source, -1, axis=1), speeds)
            return advected + KERNEL_STEP * kernel_term
        explicit = lax.map(block_update, (kernel_tiles, tile_cols, current.reshape(RBLK, TILE, NX, -1), speed_blocks))
        explicit = explicit.reshape(current.shape)
        moments = jnp.dot(weighted, explicit.reshape(V, -1), precision=PRECISE)
        coeffs = jnp.dot(inverse, moments, precision=PRECISE)
        equilibrium = jnp.dot(invariants.T, coeffs, precision=PRECISE).reshape(current.shape)
        current = explicit - relax_share[None] * (explicit - equilibrium)
    return current
```

```python
import functools

import jax
import jax.numpy as jnp
from jax import lax
from jax.experimental import pallas as pl
from jax.experimental.pallas import tpu as pltpu
from jax.sharding import PartitionSpec as P

Q = 16
TILE = 128
NZ = 4
STEPS = 2
V = 4096
RBLK = 32
CHUNK = 256
PART = 128
COURANT_SCALE = 0.3
KERNEL_STEP = 0.5
MESH = pl.DeviceIdType.MESH
F32 = jnp.float32
BF16 = jnp.bfloat16


def speeds(node_index):
    middle = (Q - 1) / 2.0
    speed_x = ((node_index & (Q - 1)).astype(F32) - middle) / middle
    speed_y = ((lax.shift_right_logical(node_index, 4) & (Q - 1)).astype(F32) - middle) / middle
    speed_z = (lax.shift_right_logical(node_index, 8).astype(F32) - middle) / middle
    return speed_x, speed_y, speed_z


def row_speeds(first, rows):
    return speeds(first + lax.broadcasted_iota(jnp.int32, (rows, 1), 0))


def vert_plan(me, count, chunks):
    if count == 4:
        x, y = lax.rem(me, 2), lax.div(me, 2)
        px, py, pd = y * 2 + (1 - x), (1 - y) * 2 + x, 3 - me
        half = chunks // 2
        first = list(range(half))
        second = list(range(half, chunks))
        to_x = [(c, px, me, c) for c in first + second]
        to_y = [(chunks + c, py, me, c) for c in second + first]
        own = [send for pair in zip(to_x, to_y) for send in pair]
        from_x = [(c, px, c) for c in first + second]
        from_y = [(chunks + c, py, c) for c in second + first]
        arrivals = [item for pair in zip(from_x, from_y) for item in pair]
        forwards = {}
        for c in first:
            forwards[c] = (2 * chunks + c, py, px, c)
        for c in second:
            forwards[chunks + c] = (2 * chunks + c, px, py, c)
        late = [c for pair in zip(first, second) for c in pair]
        arrivals += [(2 * chunks + c, pd, c) for c in late]
        return own, arrivals, forwards
    own, arrivals = [], []
    for p in range(1, count):
        for c in range(chunks):
            key = (p - 1) * chunks + c
            own.append((key, lax.rem(me + p, count), me, c))
            arrivals.append((key, lax.rem(me + count - p, count), c))
    return own, arrivals, {}


def kernel(
    count, slabs, place_ref, tiles_ref, dist_ref, relax_ref, weight_ref, out_ref,
    tiles, dense, state, acc, gathered, plane_out, plane_in, mom_out, mom_in, gram_out, gram_in,
    weights2, tile_sem, vert_send, vert_recv, plane_send, plane_recv, mom_send, mom_recv,
    gram_send, gram_recv,
):
    rows, cells = state.shape
    chunks = rows // CHUNK
    row_blocks = rows // TILE
    listed = tiles_ref.shape[2] // TILE
    me = lax.axis_index("vert")
    slab = lax.axis_index("gx")
    above = lax.rem(slab + 1, slabs)
    below = lax.rem(slab + slabs - 1, slabs)
    first_node = me * rows

    loads = [
        pltpu.make_async_copy(
            tiles_ref.at[:, :, pl.ds(j * TILE, TILE)], tiles.at[j], tile_sem.at[j]
        )
        for j in range(listed)
    ]
    for load in loads:
        load.start()

    barrier = pltpu.get_barrier_semaphore()
    for p in range(1, count):
        pl.semaphore_signal(
            barrier, inc=1, device_id=(slab, lax.rem(me + p, count)), device_id_type=MESH
        )
    for other in (below, above):
        pl.semaphore_signal(barrier, inc=1, device_id=(other, me), device_id_type=MESH)
    pl.semaphore_wait(barrier, count + 1)

    own, arrivals, forwards = vert_plan(me, count, chunks)
    pending = []

    def vert_copy(step, key, target, block, chunk):
        where = gathered.at[step, block * chunks + chunk]
        return pltpu.make_async_remote_copy(
            src_ref=where, dst_ref=where, send_sem=vert_send.at[step, key],
            recv_sem=vert_recv.at[step, key], device_id=(slab, target), device_id_type=MESH,
        )

    def plane_copy(step, side):
        return pltpu.make_async_remote_copy(
            src_ref=plane_out.at[step, side], dst_ref=plane_in.at[step, side],
            send_sem=plane_send.at[step, side], recv_sem=plane_recv.at[step, side],
            device_id=(above if side == 1 else below, me), device_id_type=MESH,
        )

    def small_copy(out, into, send, recv, p):
        return pltpu.make_async_remote_copy(
            src_ref=out, dst_ref=into, send_sem=send, recv_sem=recv,
            device_id=(slab, lax.rem(me + p, count)), device_id_type=MESH,
        )

    def publish(step, base, part):
        chunk, inner = base // CHUNK, base % CHUNK
        gathered[step, me * chunks + chunk, pl.ds(inner, PART), :] = part.astype(BF16)
        groups = part.reshape(PART // Q, 2, Q // 2, cells)
        for side in range(2):
            plane_out[step, side, pl.ds(base // 2, PART // 2), :] = (
                groups[:, side].reshape(PART // 2, cells).astype(BF16)
            )

    def send_all(step):
        for key, target, block, chunk in own:
            copy = vert_copy(step, key, target, block, chunk)
            copy.start()
            pending.append(copy)
        for side in range(2):
            copy = plane_copy(step, side)
            copy.start()
            pending.append(copy)

    for base in range(0, rows, PART):
        left = dist_ref[pl.ds(2 * base, PART, stride=2), :]
        right = dist_ref[pl.ds(2 * base + 1, PART, stride=2), :]
        part = jnp.concatenate([left, right], axis=1)
        state[pl.ds(base, PART), :] = part
        publish(0, base, part)
    send_all(0)

    lane_node = first_node + lax.broadcasted_iota(jnp.int32, (8, rows), 1)
    kind = lax.broadcasted_iota(jnp.int32, (8, rows), 0)
    sx, sy, sz = speeds(lane_node)
    kinds = [jnp.ones_like(sx), sx, sy, sz, sx * sx + sy * sy + sz * sz]
    invariants = jnp.zeros_like(sx)
    for k, row in enumerate(kinds):
        invariants = jnp.where(kind == k, row, invariants)
    weighted = invariants * weight_ref[...]
    high = weighted.astype(BF16).astype(F32)
    weights2[...] = jnp.concatenate([high, weighted - high], axis=0).astype(BF16)
    for l in range(5):
        column = jnp.sum(weighted * kinds[l], axis=1, keepdims=True)
        gram_out[l] = jnp.broadcast_to(column, (8, 128))
    for p in range(1, count):
        copy = small_copy(
            gram_out, gram_in.at[p - 1], gram_send.at[p - 1], gram_recv.at[p - 1], p
        )
        copy.start()
        pending.append(copy)

    tiles[listed] = jnp.zeros((row_blocks, TILE, TILE), BF16)
    for load in loads:
        load.wait()
    per_chunk = CHUNK // TILE

    def expand(index, carry):
        k, r = lax.div(index, row_blocks), lax.rem(index, row_blocks)
        for b in range(per_chunk):
            place = place_ref[r, k * per_chunk + b]
            dense[k, pl.ds(pl.multiple_of(r * TILE, TILE), TILE), pl.ds(b * TILE, TILE)] = tiles[
                place, r
            ]
        return carry

    lax.fori_loop(0, (V // CHUNK) * row_blocks, expand, 0, unroll=4)

    def advect(step):
        def one(i, carry):
            base = pl.multiple_of(i * PART, PART)
            source = state[pl.ds(base, PART), :]
            sides = [
                plane_in[step, side, pl.ds(pl.multiple_of(i * (PART // 2), PART // 2), PART // 2), :]
                .astype(F32)
                .reshape(PART // Q, 1, Q // 2, cells)
                for side in range(2)
            ]
            upwind_x = jnp.concatenate(sides, axis=1).reshape(PART, cells)
            px, py, pz = [COURANT_SCALE * s for s in row_speeds(first_node + base, PART)]
            z_index = lax.broadcasted_iota(jnp.int32, (PART, cells), 1) & (NZ - 1)
            lower_y = pltpu.roll(source, NZ, 1)
            upper_y = pltpu.roll(source, cells - NZ, 1)
            lower_z = jnp.where(
                z_index == 0, pltpu.roll(source, cells + 1 - NZ, 1), pltpu.roll(source, 1, 1)
            )
            upper_z = jnp.where(
                z_index == NZ - 1, pltpu.roll(source, NZ - 1, 1), pltpu.roll(source, cells - 1, 1)
            )
            flux = jnp.abs(px) * (source - upwind_x)
            flux += jnp.maximum(py, 0.0) * (source - lower_y) + jnp.minimum(py, 0.0) * (
                upper_y - source
            )
            flux += jnp.maximum(pz, 0.0) * (source - lower_z) + jnp.minimum(pz, 0.0) * (
                upper_z - source
            )
            acc[pl.ds(base, PART), :] = source - flux
            return carry

        lax.fori_loop(0, rows // PART, one, 0)

    def multiply(step, index):
        def one(i, carry):
            here = pl.ds(pl.multiple_of(i * CHUNK, CHUNK), CHUNK)
            acc[here, :] += KERNEL_STEP * jnp.dot(
                dense[index, here, :], gathered[step, index], preferred_element_type=F32
            )
            return carry

        lax.fori_loop(0, rows // CHUNK, one, 0, unroll=True)

    share = relax_ref[...] / (1.0 + relax_ref[...])
    inverse = None

    for step in range(STEPS):
        forwarded = 0

        def arrive(item, step=step):
            key, block, chunk = item
            vert_copy(step, key, me, block, chunk).wait_recv()
            if key in forwards:
                copy = vert_copy(step, *forwards[key])
                copy.start()
                pending.append(copy)
            return block * chunks + chunk

        early = [item for item in arrivals if item[0] in forwards]
        rest = [item for item in arrivals if item[0] not in forwards]
        ready = [me * chunks + c for c in range(chunks)]
        for side in range(2):
            plane_copy(step, side).wait_recv()
        advect(step)
        for index in ready[: chunks // 2]:
            multiply(step, index)
        landed = [arrive(item) for item in early]
        for index in ready[chunks // 2 :] + landed:
            multiply(step, index)
        for item in rest:
            multiply(step, arrive(item))

        total = jnp.zeros((16, cells), F32)
        for base in range(0, rows, CHUNK):
            explicit = acc[pl.ds(base, CHUNK), :]
            top = explicit.astype(BF16)
            low = (explicit - top.astype(F32)).astype(BF16)
            left = weights2[:, pl.ds(base, CHUNK)]
            total += jnp.dot(left, top, preferred_element_type=F32)
            total += jnp.dot(left, low, preferred_element_type=F32)
        mom_out[step] = total[:8] + total[8:]
        for p in range(1, count):
            copy = small_copy(
                mom_out.at[step], mom_in.at[step, p - 1], mom_send.at[step, p - 1],
                mom_recv.at[step, p - 1], p,
            )
            copy.start()
            pending.append(copy)

        if inverse is None:
            gram = gram_out[...]
            for p in range(1, count):
                small_copy(
                    gram_out, gram_in.at[p - 1], gram_send.at[p - 1], gram_recv.at[p - 1], p
                ).wait_recv()
                gram += gram_in[p - 1]
            matrix = [[gram[l, k : k + 1, :] for l in range(5)] for k in range(5)]
            one, none = jnp.ones((1, 128), F32), jnp.zeros((1, 128), F32)
            inverse = [[one if k == l else none for l in range(5)] for k in range(5)]
            for k in range(5):
                scale = 1.0 / matrix[k][k]
                matrix[k] = [entry * scale for entry in matrix[k]]
                inverse[k] = [entry * scale for entry in inverse[k]]
                for r in range(5):
                    if r != k:
                        factor = matrix[r][k]
                        matrix[r] = [a - factor * b for a, b in zip(matrix[r], matrix[k])]
                        inverse[r] = [a - factor * b for a, b in zip(inverse[r], inverse[k])]
            inverse = [
                [jnp.concatenate([entry] * (cells // 128), axis=1) for entry in line]
                for line in inverse
            ]

        moments = mom_out[step]
        for p in range(1, count):
            small_copy(
                mom_out.at[step], mom_in.at[step, p - 1], mom_send.at[step, p - 1],
                mom_recv.at[step, p - 1], p,
            ).wait_recv()
            moments += mom_in[step, p - 1]
        coeffs = [
            share * sum(inverse[k][l] * moments[l : l + 1, :] for l in range(5)) for k in range(5)
        ]
        keep = 1.0 - share
        for base in range(0, rows, PART):
            vx, vy, vz = row_speeds(first_node + base, PART)
            squares = vx * vx + vy * vy + vz * vz
            equilibrium = (
                coeffs[0] + vx * coeffs[1] + vy * coeffs[2] + vz * coeffs[3] + squares * coeffs[4]
            )
            part = keep * acc[pl.ds(base, PART), :] + equilibrium
            if step + 1 < STEPS:
                state[pl.ds(base, PART), :] = part
                publish(step + 1, base, part)
            else:
                out_ref[pl.ds(2 * base, PART, stride=2), :] = part[:, :128]
                out_ref[pl.ds(2 * base + 1, PART, stride=2), :] = part[:, 128:]
        if step + 1 < STEPS:
            send_all(step + 1)

    for copy in pending:
        copy.wait_send()


def per_device(count, slabs, distribution, relax_rate, node_weight, kernel_tiles, tile_cols):
    rows, depth, cells = distribution.shape
    assert depth == 1 and cells == 256 and rows % CHUNK == 0
    row_blocks, listed = tile_cols.shape
    chunks = rows // CHUNK
    slots = jnp.arange(listed, dtype=jnp.int32)[None, :, None]
    match = tile_cols[:, :, None] == jnp.arange(RBLK, dtype=jnp.int32)[None, None, :]
    places = listed + jnp.sum(jnp.where(match, slots - listed, 0), axis=1)
    keys = 3 * chunks if count == 4 else (count - 1) * chunks
    peers = count - 1
    vmem = pl.BlockSpec(memory_space=pltpu.VMEM)
    dma = pltpu.SemaphoreType.DMA
    result = pl.pallas_call(
        functools.partial(kernel, count, slabs),
        out_shape=jax.ShapeDtypeStruct((rows * 2, 128), F32),
        in_specs=[
            pl.BlockSpec(memory_space=pltpu.SMEM),
            pl.BlockSpec(memory_space=pl.ANY),
            vmem, vmem, vmem,
        ],
        out_specs=vmem,
        scratch_shapes=[
            pltpu.VMEM((listed + 1, row_blocks, TILE, TILE), BF16),
            pltpu.VMEM((V // CHUNK, rows, CHUNK), BF16),
            pltpu.VMEM((rows, cells), F32),
            pltpu.VMEM((rows, cells), F32),
            pltpu.VMEM((STEPS, V // CHUNK, CHUNK, cells), BF16),
            pltpu.VMEM((STEPS, 2, rows // 2, cells), BF16),
            pltpu.VMEM((STEPS, 2, rows // 2, cells), BF16),
            pltpu.VMEM((STEPS, 8, cells), F32),
            pltpu.VMEM((STEPS, peers, 8, cells), F32),
            pltpu.VMEM((5, 8, 128), F32),
            pltpu.VMEM((peers, 5, 8, 128), F32),
            pltpu.VMEM((16, rows), BF16),
            dma((listed,)),
            dma((STEPS, keys)),
            dma((STEPS, keys)),
            dma((STEPS, 2)),
            dma((STEPS, 2)),
            dma((STEPS, peers)),
            dma((STEPS, peers)),
            dma((peers,)),
            dma((peers,)),
        ],
        compiler_params=pltpu.CompilerParams(
            collective_id=0, has_side_effects=True, vmem_limit_bytes=48 * 1024 * 1024
        ),
        name="bgk_steps",
    )(
        places, kernel_tiles, distribution.reshape(rows * 2, 128), relax_rate,
        node_weight.reshape(1, rows),
    )
    return result.reshape(rows, depth, cells)


def solution(mesh):
    placed = (
        P("vert", "gx", None),
        P("gx", None),
        P("vert"),
        P("vert", None, None),
        P("vert", None),
    )
    return jax.shard_map(
        functools.partial(per_device, mesh.shape["vert"], mesh.shape["gx"]),
        mesh=mesh, in_specs=placed, out_specs=P("vert", "gx", None), check_vma=False,
    )
```

```python
import functools

import jax
import jax.numpy as jnp
from jax import lax
from jax.experimental import pallas as pl
from jax.experimental.pallas import tpu as pltpu
from jax.sharding import PartitionSpec as P

Q = 16
TILE = 128
NZ = 4
STEPS = 2
HALVES = 2
V = 4096
RBLK = 32
CHUNK = 256
PART = 128
COURANT_SCALE = 0.3
KERNEL_STEP = 0.5
MESH = pl.DeviceIdType.MESH
F32 = jnp.float32
BF16 = jnp.bfloat16


def speeds(node_index):
    middle = (Q - 1) / 2.0
    speed_x = ((node_index & (Q - 1)).astype(F32) - middle) / middle
    speed_y = ((lax.shift_right_logical(node_index, 4) & (Q - 1)).astype(F32) - middle) / middle
    speed_z = (lax.shift_right_logical(node_index, 8).astype(F32) - middle) / middle
    return speed_x, speed_y, speed_z


def row_speeds(first, rows):
    return speeds(first + lax.broadcasted_iota(jnp.int32, (rows, 1), 0))


def vert_plan(me, count, chunks):
    if count == 4:
        x, y = lax.rem(me, 2), lax.div(me, 2)
        px, py, pd = y * 2 + (1 - x), (1 - y) * 2 + x, 3 - me
        half = chunks // 2
        first = list(range(half))
        second = list(range(half, chunks))
        to_x = [(c, px, me, c) for c in first + second]
        to_y = [(chunks + c, py, me, c) for c in second + first]
        own = [send for pair in zip(to_x, to_y) for send in pair]
        from_x = [(c, px, c) for c in first + second]
        from_y = [(chunks + c, py, c) for c in second + first]
        arrivals = [item for pair in zip(from_x, from_y) for item in pair]
        forwards = {}
        for c in first:
            forwards[c] = (2 * chunks + c, py, px, c)
        for c in second:
            forwards[chunks + c] = (2 * chunks + c, px, py, c)
        late = [c for pair in zip(first, second) for c in pair]
        arrivals += [(2 * chunks + c, pd, c) for c in late]
        return own, arrivals, forwards
    own, arrivals = [], []
    for p in range(1, count):
        for c in range(chunks):
            key = (p - 1) * chunks + c
            own.append((key, lax.rem(me + p, count), me, c))
            arrivals.append((key, lax.rem(me + count - p, count), c))
    return own, arrivals, {}


def kernel(
    count, slabs, cols_ref, tiles_ref, dist_ref, relax_ref, weight_ref, out_ref,
    tiles, dense, source_rows, relax, node_weight, state, acc, gathered, plane_out, plane_in,
    mom_out, mom_in, gram_out, gram_in, weights2, tile_sem, source_sem, small_sem, vert_send,
    vert_recv, plane_send, plane_recv, mom_send, mom_recv, gram_send, gram_recv,
):
    rows, cells = state.shape
    lanes = cells // HALVES
    chunks = rows // CHUNK
    row_blocks = rows // TILE
    listed = tiles_ref.shape[2] // TILE
    me = lax.axis_index("vert")
    slab = lax.axis_index("gx")
    above = lax.rem(slab + 1, slabs)
    below = lax.rem(slab + slabs - 1, slabs)
    first_node = me * rows

    barrier = pltpu.get_barrier_semaphore()
    for p in range(1, count):
        pl.semaphore_signal(
            barrier, inc=1, device_id=(slab, lax.rem(me + p, count)), device_id_type=MESH
        )
    for other in (below, above):
        pl.semaphore_signal(barrier, inc=1, device_id=(other, me), device_id_type=MESH)

    source_loads = []
    for c in range(chunks):
        span = pl.ds(HALVES * CHUNK * c, HALVES * CHUNK)
        source_loads.append(
            pltpu.make_async_copy(dist_ref.at[span, :], source_rows.at[span, :], source_sem.at[c])
        )
    small_loads = [
        pltpu.make_async_copy(weight_ref, node_weight, small_sem.at[0]),
        pltpu.make_async_copy(relax_ref, relax, small_sem.at[1]),
    ]
    loads = [
        pltpu.make_async_copy(
            tiles_ref.at[:, :, pl.ds(j * TILE, TILE)], tiles.at[j], tile_sem.at[j]
        )
        for j in range(listed)
    ]
    for load in source_loads + small_loads + loads:
        load.start()

    own, arrivals, forwards = vert_plan(me, count, chunks)
    early = [item for item in arrivals if item[0] in forwards]
    rest = [item for item in arrivals if item[0] not in forwards]
    pending = []

    def vert_copy(stage, key, target, block, chunk):
        where = gathered.at[stage, block * chunks + chunk]
        return pltpu.make_async_remote_copy(
            src_ref=where, dst_ref=where, send_sem=vert_send.at[stage, key],
            recv_sem=vert_recv.at[stage, key], device_id=(slab, target), device_id_type=MESH,
        )

    def plane_copy(stage, side):
        return pltpu.make_async_remote_copy(
            src_ref=plane_out.at[stage, side], dst_ref=plane_in.at[stage, side],
            send_sem=plane_send.at[stage, side], recv_sem=plane_recv.at[stage, side],
            device_id=(above if side == 1 else below, me), device_id_type=MESH,
        )

    def mom_copy(stage, p):
        return pltpu.make_async_remote_copy(
            src_ref=mom_out.at[stage], dst_ref=mom_in.at[stage, p - 1],
            send_sem=mom_send.at[stage, p - 1], recv_sem=mom_recv.at[stage, p - 1],
            device_id=(slab, lax.rem(me + p, count)), device_id_type=MESH,
        )

    def gram_copy(p):
        return pltpu.make_async_remote_copy(
            src_ref=gram_out, dst_ref=gram_in.at[p - 1],
            send_sem=gram_send.at[p - 1], recv_sem=gram_recv.at[p - 1],
            device_id=(slab, lax.rem(me + p, count)), device_id_type=MESH,
        )

    def start(copy):
        copy.start()
        pending.append(copy)

    def publish(stage, base, part):
        chunk, inner = base // CHUNK, base % CHUNK
        gathered[stage, me * chunks + chunk, pl.ds(inner, PART), :] = part.astype(BF16)
        groups = part.reshape(PART // Q, 2, Q // 2, lanes)
        for side in range(2):
            plane_out[stage, side, pl.ds(base // 2, PART // 2), :] = (
                groups[:, side].reshape(PART // 2, lanes).astype(BF16)
            )

    def send_own(stage):
        for item in own:
            start(vert_copy(stage, *item))

    def send_planes(stage):
        for side in range(2):
            start(plane_copy(stage, side))

    for base in range(0, rows, PART):
        if base % CHUNK == 0:
            source_loads[base // CHUNK].wait()
        for half in range(HALVES):
            part = source_rows[pl.ds(HALVES * base + half, PART, stride=HALVES), :]
            state[pl.ds(base, PART), pl.ds(half * lanes, lanes)] = part
            publish(half, base, part)
    pl.semaphore_wait(barrier, count + 1)
    send_own(0)
    for half in range(HALVES):
        send_planes(half)

    for load in small_loads:
        load.wait()
    lane_node = first_node + lax.broadcasted_iota(jnp.int32, (8, rows), 1)
    kind = lax.broadcasted_iota(jnp.int32, (8, rows), 0)
    sx, sy, sz = speeds(lane_node)
    kinds = [jnp.ones_like(sx), sx, sy, sz, sx * sx + sy * sy + sz * sz]
    invariants = jnp.zeros_like(sx)
    for k, row in enumerate(kinds):
        invariants = jnp.where(kind == k, row, invariants)
    weighted = invariants * node_weight[...]
    high = weighted.astype(BF16).astype(F32)
    weights2[...] = jnp.concatenate([high, weighted - high], axis=0).astype(BF16)
    for l in range(5):
        column = jnp.sum(weighted * kinds[l], axis=1, keepdims=True)
        gram_out[l] = jnp.broadcast_to(column, (8, lanes))
    for p in range(1, count):
        start(gram_copy(p))

    tiles[listed] = jnp.zeros((row_blocks, TILE, TILE), BF16)
    for load in loads:
        load.wait()
    per_chunk = CHUNK // TILE

    def expand(r, carry):
        columns = [cols_ref[r, j] for j in range(listed)]
        here = pl.ds(pl.multiple_of(r * TILE, TILE), TILE)
        for c in range(RBLK):
            place = listed
            for j in range(listed):
                place = jnp.where(columns[j] == c, j, place)
            dense[c // per_chunk, here, pl.ds(c % per_chunk * TILE, TILE)] = tiles[place, r]
        return carry

    lax.fori_loop(0, row_blocks, expand, 0)

    def advect(step):
        for half in range(HALVES):
            for side in range(2):
                plane_copy(step * HALVES + half, side).wait_recv()

        def one(i, carry):
            base = pl.multiple_of(i * PART, PART)
            source = state[pl.ds(base, PART), :]
            planes = pl.ds(pl.multiple_of(i * (PART // 2), PART // 2), PART // 2)
            sides = [
                jnp.concatenate(
                    [plane_in[step * HALVES + half, side, planes, :] for half in range(HALVES)],
                    axis=1,
                ).astype(F32).reshape(PART // Q, 1, Q // 2, cells)
                for side in range(2)
            ]
            upwind_x = jnp.concatenate(sides, axis=1).reshape(PART, cells)
            px, py, pz = [COURANT_SCALE * s for s in row_speeds(first_node + base, PART)]
            z_index = lax.broadcasted_iota(jnp.int32, (PART, cells), 1) & (NZ - 1)
            lower_y = pltpu.roll(source, NZ, 1)
            upper_y = pltpu.roll(source, cells - NZ, 1)
            lower_z = jnp.where(
                z_index == 0, pltpu.roll(source, cells + 1 - NZ, 1), pltpu.roll(source, 1, 1)
            )
            upper_z = jnp.where(
                z_index == NZ - 1, pltpu.roll(source, NZ - 1, 1), pltpu.roll(source, cells - 1, 1)
            )
            flux = jnp.abs(px) * (source - upwind_x)
            flux += jnp.maximum(py, 0.0) * (source - lower_y) + jnp.minimum(py, 0.0) * (
                upper_y - source
            )
            flux += jnp.maximum(pz, 0.0) * (source - lower_z) + jnp.minimum(pz, 0.0) * (
                upper_z - source
            )
            acc[pl.ds(base, PART), :] = source - flux
            return carry

        lax.fori_loop(0, rows // PART, one, 0)

    def multiply(stage, index):
        side = pl.ds(stage % HALVES * lanes, lanes)

        def one(i, carry):
            here = pl.ds(pl.multiple_of(i * CHUNK, CHUNK), CHUNK)
            acc[here, side] += KERNEL_STEP * jnp.dot(
                dense[index, here, :], gathered[stage, index], preferred_element_type=F32
            )
            return carry

        lax.fori_loop(0, rows // CHUNK, one, 0, unroll=True)

    def arrive(stage, item):
        key, block, chunk = item
        vert_copy(stage, key, me, block, chunk).wait_recv()
        if key in forwards:
            start(vert_copy(stage, *forwards[key]))

    def relay(stage):
        for item in early:
            arrive(stage, item)

    def collide(stage):
        for chunk in range(chunks):
            multiply(stage, me * chunks + chunk)
        for key, block, chunk in early:
            multiply(stage, block * chunks + chunk)
        for item in rest:
            arrive(stage, item)
            multiply(stage, item[1] * chunks + item[2])
        side = pl.ds(stage % HALVES * lanes, lanes)
        total = jnp.zeros((16, lanes), F32)
        for base in range(0, rows, CHUNK):
            explicit = acc[pl.ds(base, CHUNK), side]
            top = explicit.astype(BF16)
            low = (explicit - top.astype(F32)).astype(BF16)
            left = weights2[:, pl.ds(base, CHUNK)]
            total += jnp.dot(left, top, preferred_element_type=F32)
            total += jnp.dot(left, low, preferred_element_type=F32)
        mom_out[stage] = total[:8] + total[8:]
        for p in range(1, count):
            start(mom_copy(stage, p))

    def invert():
        gram = gram_out[...]
        for p in range(1, count):
            gram_copy(p).wait_recv()
            gram += gram_in[p - 1]
        matrix = [[gram[l, k : k + 1, :] for l in range(5)] for k in range(5)]
        one, none = jnp.ones((1, lanes), F32), jnp.zeros((1, lanes), F32)
        inverse = [[one if k == l else none for l in range(5)] for k in range(5)]
        for k in range(5):
            scale = 1.0 / matrix[k][k]
            matrix[k] = [entry * scale for entry in matrix[k]]
            inverse[k] = [entry * scale for entry in inverse[k]]
            for r in range(5):
                if r != k:
                    factor = matrix[r][k]
                    matrix[r] = [a - factor * b for a, b in zip(matrix[r], matrix[k])]
                    inverse[r] = [a - factor * b for a, b in zip(inverse[r], inverse[k])]
        return inverse

    def relax_half(stage, inverse):
        half = stage % HALVES
        side = pl.ds(half * lanes, lanes)
        rate = relax[:, side]
        share = rate / (1.0 + rate)
        moments = mom_out[stage]
        for p in range(1, count):
            mom_copy(stage, p).wait_recv()
            moments += mom_in[stage, p - 1]
        coeffs = [
            share * sum(inverse[k][l] * moments[l : l + 1, :] for l in range(5)) for k in range(5)
        ]
        keep = 1.0 - share
        for base in range(0, rows, PART):
            vx, vy, vz = row_speeds(first_node + base, PART)
            squares = vx * vx + vy * vy + vz * vz
            equilibrium = (
                coeffs[0] + vx * coeffs[1] + vy * coeffs[2] + vz * coeffs[3] + squares * coeffs[4]
            )
            part = keep * acc[pl.ds(base, PART), side] + equilibrium
            if stage + HALVES < STEPS * HALVES:
                state[pl.ds(base, PART), side] = part
                publish(stage + HALVES, base, part)
            else:
                out_ref[pl.ds(HALVES * base + half, PART, stride=HALVES), :] = part
        if stage + HALVES < STEPS * HALVES:
            send_own(stage + HALVES)
            send_planes(stage + HALVES)

    advect(0)
    inverse = invert()
    relay(0)
    send_own(1)
    collide(0)
    relay(1)
    relax_half(0, inverse)
    collide(1)
    relay(2)
    relax_half(1, inverse)
    advect(1)
    collide(2)
    relay(3)
    relax_half(2, inverse)
    collide(3)
    relax_half(3, inverse)

    for copy in pending:
        copy.wait_send()


def per_device(count, slabs, distribution, relax_rate, node_weight, kernel_tiles, tile_cols):
    rows, depth, cells = distribution.shape
    assert depth == 1 and cells == 256 and rows % CHUNK == 0
    row_blocks, listed = tile_cols.shape
    chunks = rows // CHUNK
    keys = 3 * chunks if count == 4 else (count - 1) * chunks
    peers = count - 1
    stages = STEPS * HALVES
    lanes = cells // HALVES
    vmem = pl.BlockSpec(memory_space=pltpu.VMEM)
    dma = pltpu.SemaphoreType.DMA
    result = pl.pallas_call(
        functools.partial(kernel, count, slabs),
        out_shape=jax.ShapeDtypeStruct((rows * HALVES, lanes), F32),
        in_specs=[pl.BlockSpec(memory_space=pltpu.SMEM)] + [pl.BlockSpec(memory_space=pltpu.HBM)] * 4,
        out_specs=vmem,
        scratch_shapes=[
            pltpu.VMEM((listed + 1, row_blocks, TILE, TILE), BF16),
            pltpu.VMEM((V // CHUNK, rows, CHUNK), BF16),
            pltpu.VMEM((rows * HALVES, lanes), F32),
            pltpu.VMEM((1, cells), F32),
            pltpu.VMEM((1, rows), F32),
            pltpu.VMEM((rows, cells), F32),
            pltpu.VMEM((rows, cells), F32),
            pltpu.VMEM((stages, V // CHUNK, CHUNK, lanes), BF16),
            pltpu.VMEM((stages, 2, rows // 2, lanes), BF16),
            pltpu.VMEM((stages, 2, rows // 2, lanes), BF16),
            pltpu.VMEM((stages, 8, lanes), F32),
            pltpu.VMEM((stages, peers, 8, lanes), F32),
            pltpu.VMEM((5, 8, lanes), F32),
            pltpu.VMEM((peers, 5, 8, lanes), F32),
            pltpu.VMEM((16, rows), BF16),
            dma((listed,)),
            dma((chunks,)),
            dma((2,)),
            dma((stages, keys)),
            dma((stages, keys)),
            dma((stages, 2)),
            dma((stages, 2)),
            dma((stages, peers)),
            dma((stages, peers)),
            dma((peers,)),
            dma((peers,)),
        ],
        compiler_params=pltpu.CompilerParams(
            collective_id=0, has_side_effects=True, vmem_limit_bytes=63 * 1024 * 1024
        ),
        name="bgk_steps",
    )(
        tile_cols, kernel_tiles, distribution.reshape(rows * HALVES, lanes), relax_rate,
        node_weight.reshape(1, rows),
    )
    return result.reshape(rows, depth, cells)


def solution(mesh):
    placed = (
        P("vert", "gx", None),
        P("gx", None),
        P("vert"),
        P("vert", None, None),
        P("vert", None),
    )
    return jax.shard_map(
        functools.partial(per_device, mesh.shape["vert"], mesh.shape["gx"]),
        mesh=mesh, in_specs=placed, out_specs=P("vert", "gx", None), check_vma=False,
    )
```

```python
import functools

import jax
import jax.numpy as jnp
from jax import lax
from jax.experimental import pallas as pl
from jax.experimental.pallas import tpu as pltpu
from jax.sharding import PartitionSpec as P

Q = 16
TILE = 128
NZ = 4
STEPS = 2
HALVES = 2
V = 4096
RBLK = 32
CHUNK = 256
PART = 128
COURANT_SCALE = 0.3
KERNEL_STEP = 0.5
MESH = pl.DeviceIdType.MESH
F32 = jnp.float32
BF16 = jnp.bfloat16


def speeds(node_index):
    middle = (Q - 1) / 2.0
    speed_x = ((node_index & (Q - 1)).astype(F32) - middle) / middle
    speed_y = ((lax.shift_right_logical(node_index, 4) & (Q - 1)).astype(F32) - middle) / middle
    speed_z = (lax.shift_right_logical(node_index, 8).astype(F32) - middle) / middle
    return speed_x, speed_y, speed_z


def row_speeds(first, rows):
    return speeds(first + lax.broadcasted_iota(jnp.int32, (rows, 1), 0))


def vert_plan(me, count, chunks):
    if count == 4:
        x, y = lax.rem(me, 2), lax.div(me, 2)
        px, py, pd = y * 2 + (1 - x), (1 - y) * 2 + x, 3 - me
        half = chunks // 2
        first = list(range(half))
        second = list(range(half, chunks))
        to_x = [(c, px, me, c) for c in first + second]
        to_y = [(chunks + c, py, me, c) for c in second + first]
        own = [send for pair in zip(to_x, to_y) for send in pair]
        from_x = [(c, px, c) for c in first + second]
        from_y = [(chunks + c, py, c) for c in second + first]
        arrivals = [item for pair in zip(from_x, from_y) for item in pair]
        forwards = {}
        for c in first:
            forwards[c] = (2 * chunks + c, py, px, c)
        for c in second:
            forwards[chunks + c] = (2 * chunks + c, px, py, c)
        late = [c for pair in zip(first, second) for c in pair]
        arrivals += [(2 * chunks + c, pd, c) for c in late]
        return own, arrivals, forwards
    own, arrivals = [], []
    for p in range(1, count):
        for c in range(chunks):
            key = (p - 1) * chunks + c
            own.append((key, lax.rem(me + p, count), me, c))
            arrivals.append((key, lax.rem(me + count - p, count), c))
    return own, arrivals, {}


def kernel(
    count, slabs, cols_ref, tiles_ref, dist_ref, relax_ref, weight_ref, out_ref, constant_ref,
    tiles, dense, source_rows, relax, node_weight, state, acc, gathered, plane_out, plane_in,
    mom_out, mom_in, gram_out, gram_in, weights2, tile_sem, source_sem, small_sem, vert_send,
    vert_recv, plane_send, plane_recv, mom_send, mom_recv, gram_send, gram_recv,
):
    rows, cells = state.shape
    lanes = cells // HALVES
    chunks = rows // CHUNK
    row_blocks = rows // TILE
    listed = tiles_ref.shape[2] // TILE
    me = lax.axis_index("vert")
    slab = lax.axis_index("gx")
    above = lax.rem(slab + 1, slabs)
    below = lax.rem(slab + slabs - 1, slabs)
    first_node = me * rows

    barrier = pltpu.get_barrier_semaphore()
    for p in range(1, count):
        pl.semaphore_signal(
            barrier, inc=1, device_id=(slab, lax.rem(me + p, count)), device_id_type=MESH
        )
    for other in (below, above):
        pl.semaphore_signal(barrier, inc=1, device_id=(other, me), device_id_type=MESH)

    source_loads = []
    for c in range(chunks):
        span = pl.ds(HALVES * CHUNK * c, HALVES * CHUNK)
        source_loads.append(
            pltpu.make_async_copy(dist_ref.at[span, :], source_rows.at[span, :], source_sem.at[c])
        )
    small_loads = [
        pltpu.make_async_copy(weight_ref, node_weight, small_sem.at[0]),
        pltpu.make_async_copy(relax_ref, relax, small_sem.at[1]),
    ]
    loads = [
        pltpu.make_async_copy(
            tiles_ref.at[:, :, pl.ds(j * TILE, TILE)], tiles.at[j], tile_sem.at[j]
        )
        for j in range(listed)
    ]
    for load in source_loads + small_loads + loads:
        load.start()

    own, arrivals, forwards = vert_plan(me, count, chunks)
    early = [item for item in arrivals if item[0] in forwards]
    rest = [item for item in arrivals if item[0] not in forwards]
    pending = []

    def vert_copy(stage, key, target, block, chunk):
        where = gathered.at[stage, block * chunks + chunk]
        return pltpu.make_async_remote_copy(
            src_ref=where, dst_ref=where, send_sem=vert_send.at[stage, key],
            recv_sem=vert_recv.at[stage, key], device_id=(slab, target), device_id_type=MESH,
        )

    def plane_copy(stage, side):
        return pltpu.make_async_remote_copy(
            src_ref=plane_out.at[stage, side], dst_ref=plane_in.at[stage, side],
            send_sem=plane_send.at[stage, side], recv_sem=plane_recv.at[stage, side],
            device_id=(above if side == 1 else below, me), device_id_type=MESH,
        )

    def mom_copy(stage, p):
        return pltpu.make_async_remote_copy(
            src_ref=mom_out.at[stage], dst_ref=mom_in.at[stage, p - 1],
            send_sem=mom_send.at[stage, p - 1], recv_sem=mom_recv.at[stage, p - 1],
            device_id=(slab, lax.rem(me + p, count)), device_id_type=MESH,
        )

    def gram_copy(p):
        return pltpu.make_async_remote_copy(
            src_ref=gram_out, dst_ref=gram_in.at[p - 1],
            send_sem=gram_send.at[p - 1], recv_sem=gram_recv.at[p - 1],
            device_id=(slab, lax.rem(me + p, count)), device_id_type=MESH,
        )

    def start(copy):
        copy.start()
        pending.append(copy)

    def publish_block(stage, base, part):
        chunk, inner = base // CHUNK, base % CHUNK
        gathered[stage, me * chunks + chunk, pl.ds(inner, PART), :] = part.astype(BF16)

    def publish_planes(stage, base, part):
        groups = part.reshape(PART // Q, 2, Q // 2, lanes)
        for side in range(2):
            plane_out[stage, side, pl.ds(base // 2, PART // 2), :] = (
                groups[:, side].reshape(PART // 2, lanes).astype(BF16)
            )

    def send_own(stage, items=own):
        for item in items:
            start(vert_copy(stage, *item))

    def send_planes(stage):
        for side in range(2):
            start(plane_copy(stage, side))

    for half in range(HALVES):
        for base in range(0, rows, PART):
            if half == 0 and base % CHUNK == 0:
                source_loads[base // CHUNK].wait()
            part = source_rows[pl.ds(HALVES * base + half, PART, stride=HALVES), :]
            state[pl.ds(base, PART), pl.ds(half * lanes, lanes)] = part
            publish_block(half, base, part)
        if half == 0:
            pl.semaphore_wait(barrier, count + 1)
            send_own(0)
        else:
            send_own(1, own[: len(own) // 2])
    for half in range(HALVES):
        for base in range(0, rows, PART):
            publish_planes(half, base, state[pl.ds(base, PART), pl.ds(half * lanes, lanes)])
        send_planes(half)

    for load in small_loads:
        load.wait()
    lane_node = first_node + lax.broadcasted_iota(jnp.int32, (8, rows), 1)
    kind = lax.broadcasted_iota(jnp.int32, (8, rows), 0)
    sx, sy, sz = speeds(lane_node)
    kinds = [jnp.ones_like(sx), sx, sy, sz, sx * sx + sy * sy + sz * sz]
    invariants = jnp.zeros_like(sx)
    for k, row in enumerate(kinds):
        invariants = jnp.where(kind == k, row, invariants)
    weighted = invariants * node_weight[...]
    high = weighted.astype(BF16).astype(F32)
    weights2[...] = jnp.concatenate([high, weighted - high], axis=0).astype(BF16)
    for l in range(5):
        column = jnp.sum(weighted * kinds[l], axis=1, keepdims=True)
        gram_out[l] = jnp.broadcast_to(column, (8, lanes))
    for p in range(1, count):
        start(gram_copy(p))

    tiles[listed] = jnp.zeros((row_blocks, TILE, TILE), BF16)
    for load in loads:
        load.wait()
    per_chunk = CHUNK // TILE

    def expand(r, carry):
        columns = [cols_ref[r, j] for j in range(listed)]
        here = pl.ds(pl.multiple_of(r * TILE, TILE), TILE)
        for c in range(RBLK):
            place = listed
            for j in range(listed):
                place = jnp.where(columns[j] == c, j, place)
            dense[c // per_chunk, here, pl.ds(c % per_chunk * TILE, TILE)] = tiles[place, r]
        return carry

    lax.fori_loop(0, row_blocks, expand, 0)

    def advect(step):
        for half in range(HALVES):
            for side in range(2):
                plane_copy(step * HALVES + half, side).wait_recv()

        def one(i, carry):
            base = pl.multiple_of(i * PART, PART)
            source = state[pl.ds(base, PART), :]
            planes = pl.ds(pl.multiple_of(i * (PART // 2), PART // 2), PART // 2)
            sides = [
                jnp.concatenate(
                    [plane_in[step * HALVES + half, side, planes, :] for half in range(HALVES)],
                    axis=1,
                ).astype(F32).reshape(PART // Q, 1, Q // 2, cells)
                for side in range(2)
            ]
            upwind_x = jnp.concatenate(sides, axis=1).reshape(PART, cells)
            px, py, pz = [COURANT_SCALE * s for s in row_speeds(first_node + base, PART)]
            z_index = lax.broadcasted_iota(jnp.int32, (PART, cells), 1) & (NZ - 1)
            lower_y = pltpu.roll(source, NZ, 1)
            upper_y = pltpu.roll(source, cells - NZ, 1)
            lower_z = jnp.where(
                z_index == 0, pltpu.roll(source, cells + 1 - NZ, 1), pltpu.roll(source, 1, 1)
            )
            upper_z = jnp.where(
                z_index == NZ - 1, pltpu.roll(source, NZ - 1, 1), pltpu.roll(source, cells - 1, 1)
            )
            flux = jnp.abs(px) * (source - upwind_x)
            flux += jnp.maximum(py, 0.0) * (source - lower_y) + jnp.minimum(py, 0.0) * (
                upper_y - source
            )
            flux += jnp.maximum(pz, 0.0) * (source - lower_z) + jnp.minimum(pz, 0.0) * (
                upper_z - source
            )
            acc[pl.ds(base, PART), :] = source - flux
            return carry

        lax.fori_loop(0, rows // PART, one, 0)

    def multiply(stage, indices):
        side = pl.ds(stage % HALVES * lanes, lanes)

        def one(i, carry):
            here = pl.ds(pl.multiple_of(i * CHUNK, CHUNK), CHUNK)
            total = jnp.zeros((CHUNK, lanes), F32)
            for index in indices:
                total += jnp.dot(
                    dense[index, here, :], gathered[stage, index], preferred_element_type=F32
                )
            acc[here, side] += KERNEL_STEP * total
            return carry

        lax.fori_loop(0, rows // CHUNK, one, 0, unroll=True)

    def arrive(stage, item):
        key, block, chunk = item
        vert_copy(stage, key, me, block, chunk).wait_recv()
        if key in forwards:
            start(vert_copy(stage, *forwards[key]))

    def relay(stage):
        for item in early:
            arrive(stage, item)

    def collide(stage):
        ready = [me * chunks + chunk for chunk in range(chunks)]
        multiply(stage, ready + [block * chunks + chunk for _, block, chunk in early])
        for at in range(0, len(rest), 2):
            for item in rest[at : at + 2]:
                arrive(stage, item)
            multiply(stage, [block * chunks + chunk for _, block, chunk in rest[at : at + 2]])
        side = pl.ds(stage % HALVES * lanes, lanes)
        total = jnp.zeros((16, lanes), F32)
        for base in range(0, rows, CHUNK):
            explicit = acc[pl.ds(base, CHUNK), side]
            top = explicit.astype(BF16)
            low = (explicit - top.astype(F32)).astype(BF16)
            left = weights2[:, pl.ds(base, CHUNK)]
            total += jnp.dot(left, top, preferred_element_type=F32)
            total += jnp.dot(left, low, preferred_element_type=F32)
        mom_out[stage] = total[:8] + total[8:]
        for p in range(1, count):
            start(mom_copy(stage, p))

    def invert():
        gram = gram_out[...]
        for p in range(1, count):
            gram_copy(p).wait_recv()
            gram += gram_in[p - 1]
        matrix = [[gram[l, k : k + 1, :] for l in range(5)] for k in range(5)]
        one, none = jnp.ones((1, lanes), F32), jnp.zeros((1, lanes), F32)
        inverse = [[one if k == l else none for l in range(5)] for k in range(5)]
        for k in range(5):
            scale = 1.0 / matrix[k][k]
            matrix[k] = [entry * scale for entry in matrix[k]]
            inverse[k] = [entry * scale for entry in inverse[k]]
            for r in range(5):
                if r != k:
                    factor = matrix[r][k]
                    matrix[r] = [a - factor * b for a, b in zip(matrix[r], matrix[k])]
                    inverse[r] = [a - factor * b for a, b in zip(inverse[r], inverse[k])]
        return inverse

    def relax_half(stage, inverse):
        half = stage % HALVES
        side = pl.ds(half * lanes, lanes)
        rate = relax[:, side]
        share = rate / (1.0 + rate)
        moments = mom_out[stage]
        for p in range(1, count):
            mom_copy(stage, p).wait_recv()
            moments += mom_in[stage, p - 1]
        coeffs = [
            share * sum(inverse[k][l] * moments[l : l + 1, :] for l in range(5)) for k in range(5)
        ]
        keep = 1.0 - share
        last = stage + HALVES >= STEPS * HALVES
        if last:
            constant_ref[:, side] = coeffs[0]
        for base in range(0, rows, PART):
            vx, vy, vz = row_speeds(first_node + base, PART)
            squares = vx * vx + vy * vy + vz * vz
            part = keep * acc[pl.ds(base, PART), side]
            part += vx * coeffs[1] + vy * coeffs[2] + vz * coeffs[3] + squares * coeffs[4]
            if last:
                out_ref[pl.ds(HALVES * base + half, PART, stride=HALVES), :] = part
            else:
                part += coeffs[0]
                state[pl.ds(base, PART), side] = part
                publish_block(stage + HALVES, base, part)
        if not last:
            send_own(stage + HALVES)
            for base in range(0, rows, PART):
                publish_planes(stage + HALVES, base, state[pl.ds(base, PART), side])
            send_planes(stage + HALVES)

    relay(0)
    send_own(1, own[len(own) // 2 :])
    advect(0)
    collide(0)
    relay(1)
    inverse = invert()
    relax_half(0, inverse)
    collide(1)
    relay(2)
    relax_half(1, inverse)
    advect(1)
    collide(2)
    relay(3)
    relax_half(2, inverse)
    collide(3)
    relax_half(3, inverse)

    for copy in pending:
        copy.wait_send()


def per_device(count, slabs, distribution, relax_rate, node_weight, kernel_tiles, tile_cols):
    rows, depth, cells = distribution.shape
    assert depth == 1 and cells == 256 and rows % CHUNK == 0
    row_blocks, listed = tile_cols.shape
    chunks = rows // CHUNK
    keys = 3 * chunks if count == 4 else (count - 1) * chunks
    peers = count - 1
    stages = STEPS * HALVES
    lanes = cells // HALVES
    vmem = pl.BlockSpec(memory_space=pltpu.VMEM)
    dma = pltpu.SemaphoreType.DMA
    result, constant = pl.pallas_call(
        functools.partial(kernel, count, slabs),
        out_shape=(
            jax.ShapeDtypeStruct((rows * HALVES, lanes), F32),
            jax.ShapeDtypeStruct((1, cells), F32),
        ),
        in_specs=[pl.BlockSpec(memory_space=pltpu.SMEM)] + [pl.BlockSpec(memory_space=pltpu.HBM)] * 4,
        out_specs=(vmem, vmem),
        scratch_shapes=[
            pltpu.VMEM((listed + 1, row_blocks, TILE, TILE), BF16),
            pltpu.VMEM((V // CHUNK, rows, CHUNK), BF16),
            pltpu.VMEM((rows * HALVES, lanes), F32),
            pltpu.VMEM((1, cells), F32),
            pltpu.VMEM((1, rows), F32),
            pltpu.VMEM((rows, cells), F32),
            pltpu.VMEM((rows, cells), F32),
            pltpu.VMEM((stages, V // CHUNK, CHUNK, lanes), BF16),
            pltpu.VMEM((stages, 2, rows // 2, lanes), BF16),
            pltpu.VMEM((stages, 2, rows // 2, lanes), BF16),
            pltpu.VMEM((stages, 8, lanes), F32),
            pltpu.VMEM((stages, peers, 8, lanes), F32),
            pltpu.VMEM((5, 8, lanes), F32),
            pltpu.VMEM((peers, 5, 8, lanes), F32),
            pltpu.VMEM((16, rows), BF16),
            dma((listed,)),
            dma((chunks,)),
            dma((2,)),
            dma((stages, keys)),
            dma((stages, keys)),
            dma((stages, 2)),
            dma((stages, 2)),
            dma((stages, peers)),
            dma((stages, peers)),
            dma((peers,)),
            dma((peers,)),
        ],
        compiler_params=pltpu.CompilerParams(
            collective_id=0, has_side_effects=True, vmem_limit_bytes=63 * 1024 * 1024
        ),
        name="bgk_steps",
    )(
        tile_cols, kernel_tiles, distribution.reshape(rows * HALVES, lanes), relax_rate,
        node_weight.reshape(1, rows),
    )
    return result.reshape(rows, depth, cells) + constant[None]


def solution(mesh):
    placed = (
        P("vert", "gx", None),
        P("gx", None),
        P("vert"),
        P("vert", None, None),
        P("vert", None),
    )
    return jax.shard_map(
        functools.partial(per_device, mesh.shape["vert"], mesh.shape["gx"]),
        mesh=mesh, in_specs=placed, out_specs=P("vert", "gx", None), check_vma=False,
    )
```

```python
import functools

import jax
import jax.numpy as jnp
from jax import lax
from jax.experimental import pallas as pl
from jax.experimental.pallas import tpu as pltpu
from jax.sharding import PartitionSpec as P

Q = 16
TILE = 128
NZ = 4
STEPS = 2
HALVES = 2
V = 4096
RBLK = 32
CHUNK = 256
PART = 128
COURANT_SCALE = 0.3
KERNEL_STEP = 0.5
MESH = pl.DeviceIdType.MESH
F32 = jnp.float32
BF16 = jnp.bfloat16


def speeds(node_index):
    middle = (Q - 1) / 2.0
    speed_x = ((node_index & (Q - 1)).astype(F32) - middle) / middle
    speed_y = ((lax.shift_right_logical(node_index, 4) & (Q - 1)).astype(F32) - middle) / middle
    speed_z = (lax.shift_right_logical(node_index, 8).astype(F32) - middle) / middle
    return speed_x, speed_y, speed_z


def row_speeds(first, rows):
    return speeds(first + lax.broadcasted_iota(jnp.int32, (rows, 1), 0))


def vert_plan(me, count, chunks):
    if count == 4:
        x, y = lax.rem(me, 2), lax.div(me, 2)
        px, py, pd = y * 2 + (1 - x), (1 - y) * 2 + x, 3 - me
        half = chunks // 2
        first = list(range(half))
        second = list(range(half, chunks))
        to_x = [(c, px, me, c) for c in first + second]
        to_y = [(chunks + c, py, me, c) for c in second + first]
        own = [send for pair in zip(to_x, to_y) for send in pair]
        from_x = [(c, px, c) for c in first + second]
        from_y = [(chunks + c, py, c) for c in second + first]
        arrivals = [item for pair in zip(from_x, from_y) for item in pair]
        forwards = {}
        for c in first:
            forwards[c] = (2 * chunks + c, py, px, c)
        for c in second:
            forwards[chunks + c] = (2 * chunks + c, px, py, c)
        late = [c for pair in zip(first, second) for c in pair]
        arrivals += [(2 * chunks + c, pd, c) for c in late]
        return own, arrivals, forwards
    own, arrivals = [], []
    for p in range(1, count):
        for c in range(chunks):
            key = (p - 1) * chunks + c
            own.append((key, lax.rem(me + p, count), me, c))
            arrivals.append((key, lax.rem(me + count - p, count), c))
    return own, arrivals, {}


def kernel(
    count, slabs, cols_ref, tiles_ref, dist_ref, relax_ref, weight_ref, out_ref, constant_ref,
    tiles, dense, source_rows, relax, node_weight, state, acc, gathered, plane_out, plane_in,
    mom_out, mom_in, gram_out, gram_in, weights2,
    spread, node_table, coeff_rows, tile_sem, source_sem, small_sem, vert_send,
    vert_recv, plane_send, plane_recv, mom_send, mom_recv, gram_send, gram_recv,
):
    rows, cells = state.shape
    lanes = cells // HALVES
    chunks = rows // CHUNK
    row_blocks = rows // TILE
    listed = tiles_ref.shape[2] // TILE
    me = lax.axis_index("vert")
    slab = lax.axis_index("gx")
    above = lax.rem(slab + 1, slabs)
    below = lax.rem(slab + slabs - 1, slabs)
    first_node = me * rows

    barrier = pltpu.get_barrier_semaphore()
    for p in range(1, count):
        pl.semaphore_signal(
            barrier, inc=1, device_id=(slab, lax.rem(me + p, count)), device_id_type=MESH
        )
    for other in (below, above):
        pl.semaphore_signal(barrier, inc=1, device_id=(other, me), device_id_type=MESH)

    source_loads = []
    for c in range(chunks):
        span = pl.ds(HALVES * CHUNK * c, HALVES * CHUNK)
        source_loads.append(
            pltpu.make_async_copy(dist_ref.at[span, :], source_rows.at[span, :], source_sem.at[c])
        )
    small_loads = [
        pltpu.make_async_copy(weight_ref, node_weight, small_sem.at[0]),
        pltpu.make_async_copy(relax_ref, relax, small_sem.at[1]),
    ]
    loads = [
        pltpu.make_async_copy(
            tiles_ref.at[:, :, pl.ds(j * TILE, TILE)], tiles.at[j], tile_sem.at[j]
        )
        for j in range(listed)
    ]
    for load in source_loads + small_loads + loads:
        load.start()

    own, arrivals, forwards = vert_plan(me, count, chunks)
    early = [item for item in arrivals if item[0] in forwards]
    rest = [item for item in arrivals if item[0] not in forwards]
    pending = []

    def vert_copy(stage, key, target, block, chunk):
        where = gathered.at[stage, block * chunks + chunk]
        return pltpu.make_async_remote_copy(
            src_ref=where, dst_ref=where, send_sem=vert_send.at[stage, key],
            recv_sem=vert_recv.at[stage, key], device_id=(slab, target), device_id_type=MESH,
        )

    def plane_copy(stage, side):
        return pltpu.make_async_remote_copy(
            src_ref=plane_out.at[stage, side], dst_ref=plane_in.at[stage, side],
            send_sem=plane_send.at[stage, side], recv_sem=plane_recv.at[stage, side],
            device_id=(above if side == 1 else below, me), device_id_type=MESH,
        )

    def mom_copy(stage, p):
        return pltpu.make_async_remote_copy(
            src_ref=mom_out.at[stage], dst_ref=mom_in.at[stage, p - 1],
            send_sem=mom_send.at[stage, p - 1], recv_sem=mom_recv.at[stage, p - 1],
            device_id=(slab, lax.rem(me + p, count)), device_id_type=MESH,
        )

    def gram_copy(p):
        return pltpu.make_async_remote_copy(
            src_ref=gram_out, dst_ref=gram_in.at[p - 1],
            send_sem=gram_send.at[p - 1], recv_sem=gram_recv.at[p - 1],
            device_id=(slab, lax.rem(me + p, count)), device_id_type=MESH,
        )

    def start(copy):
        copy.start()
        pending.append(copy)

    def publish_block(stage, base, part):
        chunk, inner = base // CHUNK, base % CHUNK
        gathered[stage, me * chunks + chunk, pl.ds(inner, PART), :] = part.astype(BF16)

    def publish_planes(stage, base, part):
        groups = part.reshape(PART // Q, 2, Q // 2, lanes)
        for side in range(2):
            plane_out[stage, side, pl.ds(base // 2, PART // 2), :] = (
                groups[:, side].reshape(PART // 2, lanes).astype(BF16)
            )

    def send_own(stage, items=own):
        for item in items:
            start(vert_copy(stage, *item))

    def send_planes(stage):
        for side in range(2):
            start(plane_copy(stage, side))

    for half in range(HALVES):
        for base in range(0, rows, PART):
            if half == 0 and base % CHUNK == 0:
                source_loads[base // CHUNK].wait()
            part = source_rows[pl.ds(HALVES * base + half, PART, stride=HALVES), :]
            state[pl.ds(base, PART), pl.ds(half * lanes, lanes)] = part
            publish_block(half, base, part)
        if half == 0:
            pl.semaphore_wait(barrier, count + 1)
            send_own(0)
        else:
            send_own(1, own[: len(own) // 2])
    for half in range(HALVES):
        for base in range(0, rows, PART):
            publish_planes(half, base, state[pl.ds(base, PART), pl.ds(half * lanes, lanes)])
        send_planes(half)

    for load in small_loads:
        load.wait()
    lane_node = first_node + lax.broadcasted_iota(jnp.int32, (8, rows), 1)
    kind = lax.broadcasted_iota(jnp.int32, (8, rows), 0)
    sx, sy, sz = speeds(lane_node)
    kinds = [jnp.ones_like(sx), sx, sy, sz, sx * sx + sy * sy + sz * sz]
    invariants = jnp.zeros_like(sx)
    for k, row in enumerate(kinds):
        invariants = jnp.where(kind == k, row, invariants)
    weighted = invariants * node_weight[...]
    high = weighted.astype(BF16).astype(F32)
    weights2[...] = jnp.concatenate([high, weighted - high], axis=0).astype(BF16)
    for l in range(5):
        column = jnp.sum(weighted * kinds[l], axis=1, keepdims=True)
        gram_out[l] = jnp.broadcast_to(column, (8, lanes))
    for p in range(1, count):
        start(gram_copy(p))

    tiles[listed] = jnp.zeros((row_blocks, TILE, TILE), BF16)
    for load in loads:
        load.wait()
    per_chunk = CHUNK // TILE

    def expand(r, carry):
        columns = [cols_ref[r, j] for j in range(listed)]
        here = pl.ds(pl.multiple_of(r * TILE, TILE), TILE)
        for c in range(RBLK):
            place = listed
            for j in range(listed):
                place = jnp.where(columns[j] == c, j, place)
            dense[c // per_chunk, here, pl.ds(c % per_chunk * TILE, TILE)] = tiles[place, r]
        return carry

    lax.fori_loop(0, row_blocks, expand, 0)

    def advect(step):
        for half in range(HALVES):
            for side in range(2):
                plane_copy(step * HALVES + half, side).wait_recv()

        def one(i, carry):
            base = pl.multiple_of(i * PART, PART)
            source = state[pl.ds(base, PART), :]
            planes = pl.ds(pl.multiple_of(i * (PART // 2), PART // 2), PART // 2)
            sides = [
                jnp.concatenate(
                    [plane_in[step * HALVES + half, side, planes, :] for half in range(HALVES)],
                    axis=1,
                ).astype(F32).reshape(PART // Q, 1, Q // 2, cells)
                for side in range(2)
            ]
            upwind_x = jnp.concatenate(sides, axis=1).reshape(PART, cells)
            px, py, pz = [COURANT_SCALE * s for s in row_speeds(first_node + base, PART)]
            z_index = lax.broadcasted_iota(jnp.int32, (PART, cells), 1) & (NZ - 1)
            lower_y = pltpu.roll(source, NZ, 1)
            upper_y = pltpu.roll(source, cells - NZ, 1)
            lower_z = jnp.where(
                z_index == 0, pltpu.roll(source, cells + 1 - NZ, 1), pltpu.roll(source, 1, 1)
            )
            upper_z = jnp.where(
                z_index == NZ - 1, pltpu.roll(source, NZ - 1, 1), pltpu.roll(source, cells - 1, 1)
            )
            flux = jnp.abs(px) * (source - upwind_x)
            flux += jnp.maximum(py, 0.0) * (source - lower_y) + jnp.minimum(py, 0.0) * (
                upper_y - source
            )
            flux += jnp.maximum(pz, 0.0) * (source - lower_z) + jnp.minimum(pz, 0.0) * (
                upper_z - source
            )
            if step == 0:
                acc[pl.ds(base, PART), :] = source - flux
            else:
                shift = jnp.dot(
                    spread[pl.ds(base, PART), :], coeff_rows[...],
                    precision=lax.Precision.HIGHEST, preferred_element_type=F32,
                )
                result = source - flux + shift
                acc[pl.ds(base, PART), pl.ds(0, lanes)] += result[:, :lanes]
                acc[pl.ds(base, PART), pl.ds(lanes, cells - lanes)] = result[:, lanes:]
            return carry

        lax.fori_loop(0, rows // PART, one, 0)

    def multiply(stage, indices, fresh=False):
        side = pl.ds(stage % HALVES * lanes, lanes)

        def one(i, carry):
            here = pl.ds(pl.multiple_of(i * CHUNK, CHUNK), CHUNK)
            total = jnp.zeros((CHUNK, lanes), F32)
            for index in indices:
                total += jnp.dot(
                    dense[index, here, :], gathered[stage, index], preferred_element_type=F32
                )
            if fresh:
                acc[here, side] = KERNEL_STEP * total
            else:
                acc[here, side] += KERNEL_STEP * total
            return carry

        lax.fori_loop(0, rows // CHUNK, one, 0, unroll=True)

    def arrive(stage, item):
        key, block, chunk = item
        vert_copy(stage, key, me, block, chunk).wait_recv()
        if key in forwards:
            start(vert_copy(stage, *forwards[key]))

    def relay(stage):
        for item in early:
            arrive(stage, item)

    def kernel_term(stage, fresh=False):
        ready = [me * chunks + chunk for chunk in range(chunks)]
        multiply(stage, ready + [block * chunks + chunk for _, block, chunk in early], fresh)
        for at in range(0, len(rest), 2):
            for item in rest[at : at + 2]:
                arrive(stage, item)
            multiply(stage, [block * chunks + chunk for _, block, chunk in rest[at : at + 2]])

    def send_moments(stage):
        side = pl.ds(stage % HALVES * lanes, lanes)
        total = jnp.zeros((16, lanes), F32)
        for base in range(0, rows, CHUNK):
            explicit = acc[pl.ds(base, CHUNK), side]
            top = explicit.astype(BF16)
            low = (explicit - top.astype(F32)).astype(BF16)
            left = weights2[:, pl.ds(base, CHUNK)]
            total += jnp.dot(left, top, preferred_element_type=F32)
            total += jnp.dot(left, low, preferred_element_type=F32)
        mom_out[stage] = total[:8] + total[8:]
        for p in range(1, count):
            start(mom_copy(stage, p))

    def spread_invariants():
        lane = lax.broadcasted_iota(jnp.int32, (CHUNK, TILE), 1)
        node = lax.broadcasted_iota(jnp.int32, (CHUNK, TILE), 0)
        which = lane & 7
        tx, ty, _ = speeds(node)
        flat = jnp.where(which == 0, 1.0, 0.0)
        flat = jnp.where(which == 1, tx, jnp.where(which == 2, ty, flat))
        flat = jnp.where(which == 4, tx * tx + ty * ty, flat)
        first_z = jnp.where(which == 3, 1.0, 0.0)
        second_z = jnp.where(which == 4, 1.0, 0.0)
        middle = (Q - 1) / 2.0
        for k in range(V // CHUNK):
            tz = (k - middle) / middle
            table = flat + tz * first_z + (tz * tz) * second_z
            top = table.astype(BF16).astype(F32)
            table = jnp.where(lane < 8, top, jnp.where(lane < 16, table - top, 0.0))
            node_table[k] = table.astype(BF16)

        def one(i, carry):
            here = pl.ds(pl.multiple_of(i * CHUNK, CHUNK), CHUNK)
            total = jnp.zeros((CHUNK, TILE), F32)
            for k in range(V // CHUNK):
                total += jnp.dot(
                    dense[k, here, :], node_table[k], preferred_element_type=F32
                )
            spread[here, :] = total
            return carry

        lax.fori_loop(0, rows // CHUNK, one, 0)

    def publish_scaled(stage):
        side = pl.ds(stage % HALVES * lanes, lanes)
        keep = 1.0 / (1.0 + relax[:, side])
        for base in range(0, rows, PART):
            publish_block(stage + HALVES, base, keep * acc[pl.ds(base, PART), side])
        send_own(stage + HALVES)

    def invert():
        gram = gram_out[...]
        for p in range(1, count):
            gram_copy(p).wait_recv()
            gram += gram_in[p - 1]
        matrix = [[gram[l, k : k + 1, :] for l in range(5)] for k in range(5)]
        one, none = jnp.ones((1, lanes), F32), jnp.zeros((1, lanes), F32)
        inverse = [[one if k == l else none for l in range(5)] for k in range(5)]
        for k in range(5):
            scale = 1.0 / matrix[k][k]
            matrix[k] = [entry * scale for entry in matrix[k]]
            inverse[k] = [entry * scale for entry in inverse[k]]
            for r in range(5):
                if r != k:
                    factor = matrix[r][k]
                    matrix[r] = [a - factor * b for a, b in zip(matrix[r], matrix[k])]
                    inverse[r] = [a - factor * b for a, b in zip(inverse[r], inverse[k])]
        return inverse

    def relax_half(stage, inverse):
        half = stage % HALVES
        side = pl.ds(half * lanes, lanes)
        rate = relax[:, side]
        share = rate / (1.0 + rate)
        moments = mom_out[stage]
        for p in range(1, count):
            mom_copy(stage, p).wait_recv()
            moments += mom_in[stage, p - 1]
        coeffs = [
            share * sum(inverse[k][l] * moments[l : l + 1, :] for l in range(5)) for k in range(5)
        ]
        keep = 1.0 - share
        last = stage + HALVES >= STEPS * HALVES
        if last:
            constant_ref[:, side] = coeffs[0]
        else:
            for k in range(5):
                for row in (k, k + 8):
                    coeff_rows[row : row + 1, side] = KERNEL_STEP * coeffs[k]
        for base in range(0, rows, PART):
            vx, vy, vz = row_speeds(first_node + base, PART)
            squares = vx * vx + vy * vy + vz * vz
            part = keep * acc[pl.ds(base, PART), side]
            part += vx * coeffs[1] + vy * coeffs[2] + vz * coeffs[3] + squares * coeffs[4]
            if last:
                out_ref[pl.ds(HALVES * base + half, PART, stride=HALVES), :] = part
            else:
                part += coeffs[0]
                state[pl.ds(base, PART), side] = part
                publish_planes(stage + HALVES, base, part)
        if not last:
            send_planes(stage + HALVES)

    relay(0)
    send_own(1, own[len(own) // 2 :])
    advect(0)
    kernel_term(0)
    publish_scaled(0)
    relay(1)
    send_moments(0)
    kernel_term(1)
    publish_scaled(1)
    send_moments(1)
    coeff_rows[...] = jnp.zeros(coeff_rows.shape, F32)
    spread_invariants()
    relay(2)
    inverse = invert()
    relax_half(0, inverse)
    relax_half(1, inverse)
    kernel_term(2, fresh=True)
    relay(3)
    advect(1)
    send_moments(2)
    kernel_term(3)
    send_moments(3)
    relax_half(2, inverse)
    relax_half(3, inverse)

    for copy in pending:
        copy.wait_send()


def per_device(count, slabs, distribution, relax_rate, node_weight, kernel_tiles, tile_cols):
    rows, depth, cells = distribution.shape
    assert depth == 1 and cells == 256 and rows % CHUNK == 0
    row_blocks, listed = tile_cols.shape
    chunks = rows // CHUNK
    keys = 3 * chunks if count == 4 else (count - 1) * chunks
    peers = count - 1
    stages = STEPS * HALVES
    lanes = cells // HALVES
    vmem = pl.BlockSpec(memory_space=pltpu.VMEM)
    dma = pltpu.SemaphoreType.DMA
    result, constant = pl.pallas_call(
        functools.partial(kernel, count, slabs),
        out_shape=(
            jax.ShapeDtypeStruct((rows * HALVES, lanes), F32),
            jax.ShapeDtypeStruct((1, cells), F32),
        ),
        in_specs=[pl.BlockSpec(memory_space=pltpu.SMEM)] + [pl.BlockSpec(memory_space=pltpu.HBM)] * 4,
        out_specs=(vmem, vmem),
        scratch_shapes=[
            pltpu.VMEM((listed + 1, row_blocks, TILE, TILE), BF16),
            pltpu.VMEM((V // CHUNK, rows, CHUNK), BF16),
            pltpu.VMEM((rows * HALVES, lanes), F32),
            pltpu.VMEM((1, cells), F32),
            pltpu.VMEM((1, rows), F32),
            pltpu.VMEM((rows, cells), F32),
            pltpu.VMEM((rows, cells), F32),
            pltpu.VMEM((stages, V // CHUNK, CHUNK, lanes), BF16),
            pltpu.VMEM((stages, 2, rows // 2, lanes), BF16),
            pltpu.VMEM((stages, 2, rows // 2, lanes), BF16),
            pltpu.VMEM((stages, 8, lanes), F32),
            pltpu.VMEM((stages, peers, 8, lanes), F32),
            pltpu.VMEM((5, 8, lanes), F32),
            pltpu.VMEM((peers, 5, 8, lanes), F32),
            pltpu.VMEM((16, rows), BF16),
            pltpu.VMEM((rows, TILE), F32),
            pltpu.VMEM((V // CHUNK, CHUNK, TILE), BF16),
            pltpu.VMEM((TILE, cells), F32),
            dma((listed,)),
            dma((chunks,)),
            dma((2,)),
            dma((stages, keys)),
            dma((stages, keys)),
            dma((stages, 2)),
            dma((stages, 2)),
            dma((stages, peers)),
            dma((stages, peers)),
            dma((peers,)),
            dma((peers,)),
        ],
        compiler_params=pltpu.CompilerParams(
            collective_id=0, has_side_effects=True, vmem_limit_bytes=63 * 1024 * 1024
        ),
        name="bgk_steps",
    )(
        tile_cols, kernel_tiles, distribution.reshape(rows * HALVES, lanes), relax_rate,
        node_weight.reshape(1, rows),
    )
    return result.reshape(rows, depth, cells) + constant[None]


def solution(mesh):
    placed = (
        P("vert", "gx", None),
        P("gx", None),
        P("vert"),
        P("vert", None, None),
        P("vert", None),
    )
    return jax.shard_map(
        functools.partial(per_device, mesh.shape["vert"], mesh.shape["gx"]),
        mesh=mesh, in_specs=placed, out_specs=P("vert", "gx", None), check_vma=False,
    )
```

```python
import functools

import jax
import jax.numpy as jnp
from jax import lax
from jax.experimental import pallas as pl
from jax.experimental.pallas import tpu as pltpu
from jax.sharding import PartitionSpec as P

Q = 16
TILE = 128
NZ = 4
STEPS = 2
HALVES = 1
SPLIT = 2
V = 4096
RBLK = 32
CHUNK = 256
PART = 128
COURANT_SCALE = 0.3
KERNEL_STEP = 0.5
MESH = pl.DeviceIdType.MESH
F32 = jnp.float32
BF16 = jnp.bfloat16


def speeds(node_index):
    middle = (Q - 1) / 2.0
    speed_x = ((node_index & (Q - 1)).astype(F32) - middle) / middle
    speed_y = ((lax.shift_right_logical(node_index, 4) & (Q - 1)).astype(F32) - middle) / middle
    speed_z = (lax.shift_right_logical(node_index, 8).astype(F32) - middle) / middle
    return speed_x, speed_y, speed_z


def row_speeds(first, rows):
    return speeds(first + lax.broadcasted_iota(jnp.int32, (rows, 1), 0))


def vert_plan(me, count, chunks):
    if count == 4:
        x, y = lax.rem(me, 2), lax.div(me, 2)
        px, py, pd = y * 2 + (1 - x), (1 - y) * 2 + x, 3 - me
        half = chunks // 2
        first = list(range(half))
        second = list(range(half, chunks))
        to_x = [(c, px, me, c) for c in first + second]
        to_y = [(chunks + c, py, me, c) for c in second + first]
        own = [send for pair in zip(to_x, to_y) for send in pair]
        from_x = [(c, px, c) for c in first + second]
        from_y = [(chunks + c, py, c) for c in second + first]
        arrivals = [item for pair in zip(from_x, from_y) for item in pair]
        forwards = {}
        for c in first:
            forwards[c] = (2 * chunks + c, py, px, c)
        for c in second:
            forwards[chunks + c] = (2 * chunks + c, px, py, c)
        late = first + second
        arrivals += [(2 * chunks + c, pd, c) for c in late]
        return own, arrivals, forwards
    own, arrivals = [], []
    for p in range(1, count):
        for c in range(chunks):
            key = (p - 1) * chunks + c
            own.append((key, lax.rem(me + p, count), me, c))
            arrivals.append((key, lax.rem(me + count - p, count), c))
    return own, arrivals, {}


def kernel(
    count, slabs, cols_ref, tiles_ref, dist_ref, relax_ref, weight_ref, out_ref, constant_ref,
    tiles, dense, source_rows, relax, node_weight, state, acc, gathered, plane_out, plane_in,
    mom_out, mom_in, gram_out, gram_in, weights2,
    spread, node_table, coeff_rows, tile_sem, source_sem, small_sem, vert_send,
    vert_recv, plane_send, plane_recv, mom_send, mom_recv, gram_send, gram_recv,
):
    rows, cells = state.shape
    lanes = cells // HALVES
    chunks = rows // CHUNK
    row_blocks = rows // TILE
    listed = tiles_ref.shape[2] // TILE
    me = lax.axis_index("vert")
    slab = lax.axis_index("gx")
    above = lax.rem(slab + 1, slabs)
    below = lax.rem(slab + slabs - 1, slabs)
    first_node = me * rows

    barrier = pltpu.get_barrier_semaphore()
    for p in range(1, count):
        pl.semaphore_signal(
            barrier, inc=1, device_id=(slab, lax.rem(me + p, count)), device_id_type=MESH
        )
    for other in (below, above):
        pl.semaphore_signal(barrier, inc=1, device_id=(other, me), device_id_type=MESH)

    source_loads = []
    for c in range(chunks):
        span = pl.ds(SPLIT * CHUNK * c, SPLIT * CHUNK)
        source_loads.append(
            pltpu.make_async_copy(dist_ref.at[span, :], source_rows.at[span, :], source_sem.at[c])
        )
    small_loads = [
        pltpu.make_async_copy(weight_ref, node_weight, small_sem.at[0]),
        pltpu.make_async_copy(relax_ref, relax, small_sem.at[1]),
    ]
    loads = [
        pltpu.make_async_copy(
            tiles_ref.at[:, :, pl.ds(j * TILE, TILE)], tiles.at[j], tile_sem.at[j]
        )
        for j in range(listed)
    ]
    for load in source_loads + small_loads + loads:
        load.start()

    own, arrivals, forwards = vert_plan(me, count, chunks)
    early = [item for item in arrivals if item[0] in forwards]
    rest = [item for item in arrivals if item[0] not in forwards]
    pending = []

    def vert_copy(stage, key, target, block, chunk):
        where = gathered.at[stage, block, pl.ds(chunk * CHUNK, CHUNK), :]
        return pltpu.make_async_remote_copy(
            src_ref=where, dst_ref=where, send_sem=vert_send.at[stage, key],
            recv_sem=vert_recv.at[stage, key], device_id=(slab, target), device_id_type=MESH,
        )

    def plane_copy(stage, side):
        return pltpu.make_async_remote_copy(
            src_ref=plane_out.at[stage, side], dst_ref=plane_in.at[stage, side],
            send_sem=plane_send.at[stage, side], recv_sem=plane_recv.at[stage, side],
            device_id=(above if side == 1 else below, me), device_id_type=MESH,
        )

    def mom_copy(stage, p):
        return pltpu.make_async_remote_copy(
            src_ref=mom_out.at[stage], dst_ref=mom_in.at[stage, p - 1],
            send_sem=mom_send.at[stage, p - 1], recv_sem=mom_recv.at[stage, p - 1],
            device_id=(slab, lax.rem(me + p, count)), device_id_type=MESH,
        )

    def gram_copy(p):
        return pltpu.make_async_remote_copy(
            src_ref=gram_out, dst_ref=gram_in.at[p - 1],
            send_sem=gram_send.at[p - 1], recv_sem=gram_recv.at[p - 1],
            device_id=(slab, lax.rem(me + p, count)), device_id_type=MESH,
        )

    def start(copy):
        copy.start()
        pending.append(copy)

    def publish_block(stage, base, part):
        gathered[stage, me, pl.ds(base, PART), :] = part.astype(BF16)

    def publish_planes(stage, base, part):
        groups = part.reshape(PART // Q, 2, Q // 2, lanes)
        for side in range(2):
            plane_out[stage, side, pl.ds(base // 2, PART // 2), :] = (
                groups[:, side].reshape(PART // 2, lanes).astype(BF16)
            )

    def send_own(stage, items=own):
        for item in items:
            start(vert_copy(stage, *item))

    def send_planes(stage):
        for side in range(2):
            start(plane_copy(stage, side))

    for base in range(0, rows, PART):
        if base % CHUNK == 0:
            source_loads[base // CHUNK].wait()
        pieces = [
            source_rows[pl.ds(SPLIT * base + piece, PART, stride=SPLIT), :]
            for piece in range(SPLIT)
        ]
        part = jnp.concatenate(pieces, axis=1)
        state[pl.ds(base, PART), :] = part
        publish_block(0, base, part)
    pl.semaphore_wait(barrier, count + 1)
    send_own(0)
    for base in range(0, rows, PART):
        publish_planes(0, base, state[pl.ds(base, PART), :])
    send_planes(0)

    for load in small_loads:
        load.wait()
    lane_node = first_node + lax.broadcasted_iota(jnp.int32, (8, rows), 1)
    kind = lax.broadcasted_iota(jnp.int32, (8, rows), 0)
    sx, sy, sz = speeds(lane_node)
    kinds = [jnp.ones_like(sx), sx, sy, sz, sx * sx + sy * sy + sz * sz]
    invariants = jnp.zeros_like(sx)
    for k, row in enumerate(kinds):
        invariants = jnp.where(kind == k, row, invariants)
    weighted = invariants * node_weight[...]
    high = weighted.astype(BF16).astype(F32)
    weights2[...] = jnp.concatenate([high, weighted - high], axis=0).astype(BF16)
    for l in range(5):
        column = jnp.sum(weighted * kinds[l], axis=1, keepdims=True)
        gram_out[l] = jnp.broadcast_to(column, (8, lanes))
    for p in range(1, count):
        start(gram_copy(p))

    tiles[listed] = jnp.zeros((row_blocks, TILE, TILE), BF16)
    for load in loads:
        load.wait()
    def expand(r, carry):
        columns = [cols_ref[r, j] for j in range(listed)]
        here = pl.ds(pl.multiple_of(r * TILE, TILE), TILE)
        for c in range(RBLK):
            place = listed
            for j in range(listed):
                place = jnp.where(columns[j] == c, j, place)
            dense[c // row_blocks, here, pl.ds(c % row_blocks * TILE, TILE)] = tiles[place, r]
        return carry

    lax.fori_loop(0, row_blocks, expand, 0)

    def advect(step):
        for half in range(HALVES):
            for side in range(2):
                plane_copy(step * HALVES + half, side).wait_recv()

        def one(i, carry):
            base = pl.multiple_of(i * PART, PART)
            source = state[pl.ds(base, PART), :]
            planes = pl.ds(pl.multiple_of(i * (PART // 2), PART // 2), PART // 2)
            sides = [
                jnp.concatenate(
                    [plane_in[step * HALVES + half, side, planes, :] for half in range(HALVES)],
                    axis=1,
                ).astype(F32).reshape(PART // Q, 1, Q // 2, cells)
                for side in range(2)
            ]
            upwind_x = jnp.concatenate(sides, axis=1).reshape(PART, cells)
            px, py, pz = [COURANT_SCALE * s for s in row_speeds(first_node + base, PART)]
            z_index = lax.broadcasted_iota(jnp.int32, (PART, cells), 1) & (NZ - 1)
            lower_y = pltpu.roll(source, NZ, 1)
            upper_y = pltpu.roll(source, cells - NZ, 1)
            lower_z = jnp.where(
                z_index == 0, pltpu.roll(source, cells + 1 - NZ, 1), pltpu.roll(source, 1, 1)
            )
            upper_z = jnp.where(
                z_index == NZ - 1, pltpu.roll(source, NZ - 1, 1), pltpu.roll(source, cells - 1, 1)
            )
            flux = jnp.abs(px) * (source - upwind_x)
            flux += jnp.maximum(py, 0.0) * (source - lower_y) + jnp.minimum(py, 0.0) * (
                upper_y - source
            )
            flux += jnp.maximum(pz, 0.0) * (source - lower_z) + jnp.minimum(pz, 0.0) * (
                upper_z - source
            )
            if step == 0:
                acc[pl.ds(base, PART), :] = source - flux
            else:
                shift = jnp.dot(
                    spread[pl.ds(base, PART), :], coeff_rows[...],
                    precision=lax.Precision.HIGHEST, preferred_element_type=F32,
                )
                acc[pl.ds(base, PART), :] += source - flux + shift
            return carry

        lax.fori_loop(0, rows // PART, one, 0)

    def multiply(stage, groups, fresh=False):
        def one(i, carry):
            here = pl.ds(pl.multiple_of(i * CHUNK, CHUNK), CHUNK)
            total = None
            for block, first, length in groups:
                span = pl.ds(first * CHUNK, length * CHUNK)
                term = jnp.dot(
                    dense[block, here, span], gathered[stage, block, span, :],
                    preferred_element_type=F32,
                )
                total = term if total is None else total + term
            if fresh:
                acc[here, :] = KERNEL_STEP * total
            else:
                acc[here, :] += KERNEL_STEP * total
            return carry

        lax.fori_loop(0, rows // CHUNK, one, 0)

    def arrive(stage, item):
        key, block, chunk = item
        vert_copy(stage, key, me, block, chunk).wait_recv()
        if key in forwards:
            start(vert_copy(stage, *forwards[key]))

    def relay(stage):
        for item in early:
            arrive(stage, item)

    def runs(items):
        found = {}
        for _, block, chunk in items:
            found.setdefault(id(block), (block, []))[1].append(chunk)
        return [(block, min(held), len(held)) for block, held in found.values()]

    def kernel_first(stage, fresh=False):
        multiply(stage, [(me, 0, chunks)] + runs(early), fresh)

    def kernel_rest(stage):
        at = 0
        while at < len(rest):
            size = chunks if at < chunks or count != 4 else chunks // 2
            part = rest[at : at + size]
            for item in part:
                arrive(stage, item)
            multiply(stage, runs(part))
            at += size

    def send_moments(stage):
        side = pl.ds(stage % HALVES * lanes, lanes)
        total = jnp.zeros((16, lanes), F32)
        for base in range(0, rows, CHUNK):
            explicit = acc[pl.ds(base, CHUNK), side]
            top = explicit.astype(BF16)
            low = (explicit - top.astype(F32)).astype(BF16)
            left = weights2[:, pl.ds(base, CHUNK)]
            total += jnp.dot(left, top, preferred_element_type=F32)
            total += jnp.dot(left, low, preferred_element_type=F32)
        mom_out[stage] = total[:8] + total[8:]
        for p in range(1, count):
            start(mom_copy(stage, p))

    def spread_invariants():
        lane = lax.broadcasted_iota(jnp.int32, (CHUNK, TILE), 1)
        node = lax.broadcasted_iota(jnp.int32, (CHUNK, TILE), 0)
        which = lane & 7
        tx, ty, _ = speeds(node)
        flat = jnp.where(which == 0, 1.0, 0.0)
        flat = jnp.where(which == 1, tx, jnp.where(which == 2, ty, flat))
        flat = jnp.where(which == 4, tx * tx + ty * ty, flat)
        first_z = jnp.where(which == 3, 1.0, 0.0)
        second_z = jnp.where(which == 4, 1.0, 0.0)
        middle = (Q - 1) / 2.0
        for k in range(V // CHUNK):
            tz = (k - middle) / middle
            table = flat + tz * first_z + (tz * tz) * second_z
            top = table.astype(BF16).astype(F32)
            table = jnp.where(lane < 8, top, jnp.where(lane < 16, table - top, 0.0))
            node_table[k] = table.astype(BF16)

        def one(i, carry):
            here = pl.ds(pl.multiple_of(i * CHUNK, CHUNK), CHUNK)
            total = jnp.zeros((CHUNK, TILE), F32)
            for k in range(V // CHUNK):
                total += jnp.dot(
                    dense[k // chunks, here, pl.ds(k % chunks * CHUNK, CHUNK)], node_table[k],
                    preferred_element_type=F32,
                )
            spread[here, :] = total
            return carry

        lax.fori_loop(0, rows // CHUNK, one, 0)

    def publish_scaled(stage):
        side = pl.ds(stage % HALVES * lanes, lanes)
        keep = 1.0 / (1.0 + relax[:, side])
        for base in range(0, rows, PART):
            publish_block(stage + HALVES, base, keep * acc[pl.ds(base, PART), side])
        send_own(stage + HALVES)

    def invert():
        gram = gram_out[...]
        for p in range(1, count):
            gram_copy(p).wait_recv()
            gram += gram_in[p - 1]
        matrix = [[gram[l, k : k + 1, :] for l in range(5)] for k in range(5)]
        one, none = jnp.ones((1, lanes), F32), jnp.zeros((1, lanes), F32)
        inverse = [[one if k == l else none for l in range(5)] for k in range(5)]
        for k in range(5):
            scale = 1.0 / matrix[k][k]
            matrix[k] = [entry * scale for entry in matrix[k]]
            inverse[k] = [entry * scale for entry in inverse[k]]
            for r in range(5):
                if r != k:
                    factor = matrix[r][k]
                    matrix[r] = [a - factor * b for a, b in zip(matrix[r], matrix[k])]
                    inverse[r] = [a - factor * b for a, b in zip(inverse[r], inverse[k])]
        return inverse

    def relax_half(stage, inverse):
        side = pl.ds(0, lanes)
        rate = relax[:, side]
        share = rate / (1.0 + rate)
        moments = mom_out[stage]
        for p in range(1, count):
            mom_copy(stage, p).wait_recv()
            moments += mom_in[stage, p - 1]
        coeffs = [
            share * sum(inverse[k][l] * moments[l : l + 1, :] for l in range(5)) for k in range(5)
        ]
        keep = 1.0 - share
        last = stage + HALVES >= STEPS * HALVES
        if last:
            constant_ref[:, side] = coeffs[0]
        else:
            for k in range(5):
                for row in (k, k + 8):
                    coeff_rows[row : row + 1, side] = KERNEL_STEP * coeffs[k]
        for base in range(0, rows, PART):
            vx, vy, vz = row_speeds(first_node + base, PART)
            squares = vx * vx + vy * vy + vz * vz
            part = keep * acc[pl.ds(base, PART), side]
            part += vx * coeffs[1] + vy * coeffs[2] + vz * coeffs[3] + squares * coeffs[4]
            if last:
                for piece in range(SPLIT):
                    out_ref[pl.ds(SPLIT * base + piece, PART, stride=SPLIT), :] = part[
                        :, piece * 128 : (piece + 1) * 128
                    ]
            else:
                part += coeffs[0]
                state[pl.ds(base, PART), side] = part
                publish_planes(stage + HALVES, base, part)
        if not last:
            send_planes(stage + HALVES)

    relay(0)
    advect(0)
    kernel_first(0)
    kernel_rest(0)
    publish_scaled(0)
    send_moments(0)
    coeff_rows[...] = jnp.zeros(coeff_rows.shape, F32)
    spread_invariants()
    inverse = invert()
    relax_half(0, inverse)
    relay(1)
    kernel_first(1, fresh=True)
    advect(1)
    kernel_rest(1)
    send_moments(1)
    relax_half(1, inverse)

    for copy in pending:
        copy.wait_send()


def per_device(count, slabs, distribution, relax_rate, node_weight, kernel_tiles, tile_cols):
    rows, depth, cells = distribution.shape
    assert depth == 1 and cells == 256 and rows % CHUNK == 0
    row_blocks, listed = tile_cols.shape
    chunks = rows // CHUNK
    keys = 3 * chunks if count == 4 else (count - 1) * chunks
    peers = count - 1
    stages = STEPS * HALVES
    lanes = cells // HALVES
    vmem = pl.BlockSpec(memory_space=pltpu.VMEM)
    dma = pltpu.SemaphoreType.DMA
    result, constant = pl.pallas_call(
        functools.partial(kernel, count, slabs),
        out_shape=(
            jax.ShapeDtypeStruct((rows * SPLIT, cells // SPLIT), F32),
            jax.ShapeDtypeStruct((1, cells), F32),
        ),
        in_specs=[pl.BlockSpec(memory_space=pltpu.SMEM)] + [pl.BlockSpec(memory_space=pltpu.HBM)] * 4,
        out_specs=(vmem, vmem),
        scratch_shapes=[
            pltpu.VMEM((listed + 1, row_blocks, TILE, TILE), BF16),
            pltpu.VMEM((V // rows, rows, rows), BF16),
            pltpu.VMEM((rows * SPLIT, cells // SPLIT), F32),
            pltpu.VMEM((1, cells), F32),
            pltpu.VMEM((1, rows), F32),
            pltpu.VMEM((rows, cells), F32),
            pltpu.VMEM((rows, cells), F32),
            pltpu.VMEM((stages, V // rows, rows, lanes), BF16),
            pltpu.VMEM((stages, 2, rows // 2, lanes), BF16),
            pltpu.VMEM((stages, 2, rows // 2, lanes), BF16),
            pltpu.VMEM((stages, 8, lanes), F32),
            pltpu.VMEM((stages, peers, 8, lanes), F32),
            pltpu.VMEM((5, 8, lanes), F32),
            pltpu.VMEM((peers, 5, 8, lanes), F32),
            pltpu.VMEM((16, rows), BF16),
            pltpu.VMEM((rows, TILE), F32),
            pltpu.VMEM((V // CHUNK, CHUNK, TILE), BF16),
            pltpu.VMEM((TILE, cells), F32),
            dma((listed,)),
            dma((chunks,)),
            dma((2,)),
            dma((stages, keys)),
            dma((stages, keys)),
            dma((stages, 2)),
            dma((stages, 2)),
            dma((stages, peers)),
            dma((stages, peers)),
            dma((peers,)),
            dma((peers,)),
        ],
        compiler_params=pltpu.CompilerParams(
            collective_id=0, has_side_effects=True, vmem_limit_bytes=63 * 1024 * 1024
        ),
        name="bgk_steps",
    )(
        tile_cols, kernel_tiles, distribution.reshape(rows * SPLIT, cells // SPLIT), relax_rate,
        node_weight.reshape(1, rows),
    )
    return result.reshape(rows, depth, cells) + constant[None]


def solution(mesh):
    placed = (
        P("vert", "gx", None),
        P("gx", None),
        P("vert"),
        P("vert", None, None),
        P("vert", None),
    )
    return jax.shard_map(
        functools.partial(per_device, mesh.shape["vert"], mesh.shape["gx"]),
        mesh=mesh, in_specs=placed, out_specs=P("vert", "gx", None), check_vma=False,
    )
```

```python
import functools

import jax
import jax.numpy as jnp
from jax import lax
from jax.experimental import pallas as pl
from jax.experimental.pallas import tpu as pltpu
from jax.sharding import PartitionSpec as P

Q = 16
TILE = 128
NZ = 4
STEPS = 2
HALVES = 2
V = 4096
RBLK = 32
CHUNK = 256
PART = 128
COURANT_SCALE = 0.3
KERNEL_STEP = 0.5
MESH = pl.DeviceIdType.MESH
F32 = jnp.float32
BF16 = jnp.bfloat16


def speeds(node_index):
    middle = (Q - 1) / 2.0
    speed_x = ((node_index & (Q - 1)).astype(F32) - middle) / middle
    speed_y = ((lax.shift_right_logical(node_index, 4) & (Q - 1)).astype(F32) - middle) / middle
    speed_z = (lax.shift_right_logical(node_index, 8).astype(F32) - middle) / middle
    return speed_x, speed_y, speed_z


def row_speeds(first, rows):
    return speeds(first + lax.broadcasted_iota(jnp.int32, (rows, 1), 0))


def vert_plan(me, count, chunks):
    if count == 4:
        x, y = lax.rem(me, 2), lax.div(me, 2)
        px, py, pd = y * 2 + (1 - x), (1 - y) * 2 + x, 3 - me
        half = chunks // 2
        first = list(range(half))
        second = list(range(half, chunks))
        to_x = [(c, px, me, c) for c in first + second]
        to_y = [(chunks + c, py, me, c) for c in second + first]
        own = [send for pair in zip(to_x, to_y) for send in pair]
        from_x = [(c, px, c) for c in first + second]
        from_y = [(chunks + c, py, c) for c in second + first]
        arrivals = [item for pair in zip(from_x, from_y) for item in pair]
        forwards = {}
        for c in first:
            forwards[c] = (2 * chunks + c, py, px, c)
        for c in second:
            forwards[chunks + c] = (2 * chunks + c, px, py, c)
        late = [c for pair in zip(first, second) for c in pair]
        arrivals += [(2 * chunks + c, pd, c) for c in late]
        return own, arrivals, forwards
    own, arrivals = [], []
    for p in range(1, count):
        for c in range(chunks):
            key = (p - 1) * chunks + c
            own.append((key, lax.rem(me + p, count), me, c))
            arrivals.append((key, lax.rem(me + count - p, count), c))
    return own, arrivals, {}


def kernel(
    count, slabs, place_ref, tiles_ref, dist_ref, relax_ref, weight_ref, out_ref, constant_ref,
    tiles, dense, source_rows, relax, node_weight, state, acc, gathered, plane_out, plane_in,
    mom_out, mom_in, gram_out, gram_in, weights2, tile_sem, source_sem, small_sem, vert_send,
    vert_recv, plane_send, plane_recv, mom_send, mom_recv, gram_send, gram_recv,
):
    rows, cells = state.shape
    lanes = cells // HALVES
    chunks = rows // CHUNK
    row_blocks = rows // TILE
    listed = tiles_ref.shape[2] // TILE
    me = lax.axis_index("vert")
    slab = lax.axis_index("gx")
    above = lax.rem(slab + 1, slabs)
    below = lax.rem(slab + slabs - 1, slabs)
    first_node = me * rows

    barrier = pltpu.get_barrier_semaphore()
    for p in range(1, count):
        pl.semaphore_signal(
            barrier, inc=1, device_id=(slab, lax.rem(me + p, count)), device_id_type=MESH
        )
    for other in (below, above):
        pl.semaphore_signal(barrier, inc=1, device_id=(other, me), device_id_type=MESH)

    source_loads = []
    for c in range(chunks):
        span = pl.ds(HALVES * CHUNK * c, HALVES * CHUNK)
        source_loads.append(
            pltpu.make_async_copy(dist_ref.at[span, :], source_rows.at[span, :], source_sem.at[c])
        )
    small_loads = [
        pltpu.make_async_copy(weight_ref, node_weight, small_sem.at[0]),
        pltpu.make_async_copy(relax_ref, relax, small_sem.at[1]),
    ]
    loads = [
        pltpu.make_async_copy(
            tiles_ref.at[:, :, pl.ds(j * TILE, TILE)], tiles.at[j], tile_sem.at[j]
        )
        for j in range(listed)
    ]
    for load in source_loads + small_loads + loads:
        load.start()

    own, arrivals, forwards = vert_plan(me, count, chunks)
    early = [item for item in arrivals if item[0] in forwards]
    rest = [item for item in arrivals if item[0] not in forwards]
    pending = []

    def vert_copy(stage, key, target, block, chunk):
        where = gathered.at[stage, block * chunks + chunk]
        return pltpu.make_async_remote_copy(
            src_ref=where, dst_ref=where, send_sem=vert_send.at[stage, key],
            recv_sem=vert_recv.at[stage, key], device_id=(slab, target), device_id_type=MESH,
        )

    def plane_copy(stage, side):
        return pltpu.make_async_remote_copy(
            src_ref=plane_out.at[stage, side], dst_ref=plane_in.at[stage, side],
            send_sem=plane_send.at[stage, side], recv_sem=plane_recv.at[stage, side],
            device_id=(above if side == 1 else below, me), device_id_type=MESH,
        )

    def mom_copy(stage, p):
        return pltpu.make_async_remote_copy(
            src_ref=mom_out.at[stage], dst_ref=mom_in.at[stage, p - 1],
            send_sem=mom_send.at[stage, p - 1], recv_sem=mom_recv.at[stage, p - 1],
            device_id=(slab, lax.rem(me + p, count)), device_id_type=MESH,
        )

    def gram_copy(p):
        return pltpu.make_async_remote_copy(
            src_ref=gram_out, dst_ref=gram_in.at[p - 1],
            send_sem=gram_send.at[p - 1], recv_sem=gram_recv.at[p - 1],
            device_id=(slab, lax.rem(me + p, count)), device_id_type=MESH,
        )

    def start(copy):
        copy.start()
        pending.append(copy)

    def publish_block(stage, base, part):
        chunk, inner = base // CHUNK, base % CHUNK
        gathered[stage, me * chunks + chunk, pl.ds(inner, PART), :] = part.astype(BF16)

    def publish_planes(stage, base, part):
        groups = part.reshape(PART // Q, 2, Q // 2, lanes)
        for side in range(2):
            plane_out[stage, side, pl.ds(base // 2, PART // 2), :] = (
                groups[:, side].reshape(PART // 2, lanes).astype(BF16)
            )

    def send_own(stage, items=own):
        for item in items:
            start(vert_copy(stage, *item))

    def send_planes(stage):
        for side in range(2):
            start(plane_copy(stage, side))

    for half in range(HALVES):
        for base in range(0, rows, PART):
            if half == 0 and base % CHUNK == 0:
                source_loads[base // CHUNK].wait()
            part = source_rows[pl.ds(HALVES * base + half, PART, stride=HALVES), :]
            state[pl.ds(base, PART), pl.ds(half * lanes, lanes)] = part
            publish_block(half, base, part)
        if half == 0:
            pl.semaphore_wait(barrier, count + 1)
            send_own(0)
        else:
            send_own(1, own[: len(own) // 2])
    for half in range(HALVES):
        for base in range(0, rows, PART):
            publish_planes(half, base, state[pl.ds(base, PART), pl.ds(half * lanes, lanes)])
        send_planes(half)

    for load in small_loads:
        load.wait()
    lane_node = first_node + lax.broadcasted_iota(jnp.int32, (8, rows), 1)
    kind = lax.broadcasted_iota(jnp.int32, (8, rows), 0)
    sx, sy, sz = speeds(lane_node)
    kinds = [jnp.ones_like(sx), sx, sy, sz, sx * sx + sy * sy + sz * sz]
    invariants = jnp.zeros_like(sx)
    for k, row in enumerate(kinds):
        invariants = jnp.where(kind == k, row, invariants)
    weighted = invariants * node_weight[...]
    high = weighted.astype(BF16).astype(F32)
    weights2[...] = jnp.concatenate([high, weighted - high], axis=0).astype(BF16)
    for l in range(5):
        column = jnp.sum(weighted * kinds[l], axis=1, keepdims=True)
        gram_out[l] = jnp.broadcast_to(column, (8, lanes))
    for p in range(1, count):
        start(gram_copy(p))

    tiles[listed] = jnp.zeros((row_blocks, TILE, TILE), BF16)
    for load in loads:
        load.wait()
    per_chunk = CHUNK // TILE

    def expand(index, carry):
        k, r = lax.div(index, row_blocks), lax.rem(index, row_blocks)
        here = pl.ds(pl.multiple_of(r * TILE, TILE), TILE)
        for b in range(per_chunk):
            place = place_ref[r, k * per_chunk + b]
            dense[k, here, pl.ds(b * TILE, TILE)] = tiles[place, r]
        return carry

    lax.fori_loop(0, (V // CHUNK) * row_blocks, expand, 0, unroll=4)

    def advect(step):
        for half in range(HALVES):
            for side in range(2):
                plane_copy(step * HALVES + half, side).wait_recv()

        def one(i, carry):
            base = pl.multiple_of(i * PART, PART)
            source = state[pl.ds(base, PART), :]
            planes = pl.ds(pl.multiple_of(i * (PART // 2), PART // 2), PART // 2)
            sides = [
                jnp.concatenate(
                    [plane_in[step * HALVES + half, side, planes, :] for half in range(HALVES)],
                    axis=1,
                ).astype(F32).reshape(PART // Q, 1, Q // 2, cells)
                for side in range(2)
            ]
            upwind_x = jnp.concatenate(sides, axis=1).reshape(PART, cells)
            px, py, pz = [COURANT_SCALE * s for s in row_speeds(first_node + base, PART)]
            z_index = lax.broadcasted_iota(jnp.int32, (PART, cells), 1) & (NZ - 1)
            lower_y = pltpu.roll(source, NZ, 1)
            upper_y = pltpu.roll(source, cells - NZ, 1)
            lower_z = jnp.where(
                z_index == 0, pltpu.roll(source, cells + 1 - NZ, 1), pltpu.roll(source, 1, 1)
            )
            upper_z = jnp.where(
                z_index == NZ - 1, pltpu.roll(source, NZ - 1, 1), pltpu.roll(source, cells - 1, 1)
            )
            flux = jnp.abs(px) * (source - upwind_x)
            flux += jnp.maximum(py, 0.0) * (source - lower_y) + jnp.minimum(py, 0.0) * (
                upper_y - source
            )
            flux += jnp.maximum(pz, 0.0) * (source - lower_z) + jnp.minimum(pz, 0.0) * (
                upper_z - source
            )
            result = source - flux
            if step == 0:
                acc[pl.ds(base, PART), :] = result
            else:
                acc[pl.ds(base, PART), pl.ds(0, lanes)] += result[:, :lanes]
                acc[pl.ds(base, PART), pl.ds(lanes, cells - lanes)] = result[:, lanes:]
            return carry

        lax.fori_loop(0, rows // PART, one, 0)

    def multiply(stage, indices, fresh=False):
        side = pl.ds(stage % HALVES * lanes, lanes)

        def one(i, carry):
            here = pl.ds(pl.multiple_of(i * CHUNK, CHUNK), CHUNK)
            total = jnp.zeros((CHUNK, lanes), F32)
            for index in indices:
                total += jnp.dot(
                    dense[index, here, :], gathered[stage, index], preferred_element_type=F32
                )
            if fresh:
                acc[here, side] = KERNEL_STEP * total
            else:
                acc[here, side] += KERNEL_STEP * total
            return carry

        lax.fori_loop(0, rows // CHUNK, one, 0, unroll=True)

    def arrive(stage, item):
        key, block, chunk = item
        vert_copy(stage, key, me, block, chunk).wait_recv()
        if key in forwards:
            start(vert_copy(stage, *forwards[key]))

    def relay(stage):
        for item in early:
            arrive(stage, item)

    def kernel_term(stage, fresh=False):
        ready = [me * chunks + chunk for chunk in range(chunks)]
        multiply(stage, ready + [block * chunks + chunk for _, block, chunk in early], fresh)
        for at in range(0, len(rest), 2):
            for item in rest[at : at + 2]:
                arrive(stage, item)
            multiply(stage, [block * chunks + chunk for _, block, chunk in rest[at : at + 2]])

    def send_moments(stage):
        side = pl.ds(stage % HALVES * lanes, lanes)
        total = jnp.zeros((16, lanes), F32)
        for base in range(0, rows, CHUNK):
            explicit = acc[pl.ds(base, CHUNK), side]
            top = explicit.astype(BF16)
            low = (explicit - top.astype(F32)).astype(BF16)
            left = weights2[:, pl.ds(base, CHUNK)]
            total += jnp.dot(left, top, preferred_element_type=F32)
            total += jnp.dot(left, low, preferred_element_type=F32)
        mom_out[stage] = total[:8] + total[8:]
        for p in range(1, count):
            start(mom_copy(stage, p))

    def invert():
        gram = gram_out[...]
        for p in range(1, count):
            gram_copy(p).wait_recv()
            gram += gram_in[p - 1]
        matrix = [[gram[l, k : k + 1, :] for l in range(5)] for k in range(5)]
        one, none = jnp.ones((1, lanes), F32), jnp.zeros((1, lanes), F32)
        inverse = [[one if k == l else none for l in range(5)] for k in range(5)]
        for k in range(5):
            scale = 1.0 / matrix[k][k]
            matrix[k] = [entry * scale for entry in matrix[k]]
            inverse[k] = [entry * scale for entry in inverse[k]]
            for r in range(5):
                if r != k:
                    factor = matrix[r][k]
                    matrix[r] = [a - factor * b for a, b in zip(matrix[r], matrix[k])]
                    inverse[r] = [a - factor * b for a, b in zip(inverse[r], inverse[k])]
        return inverse

    def relax_half(stage, inverse):
        half = stage % HALVES
        side = pl.ds(half * lanes, lanes)
        rate = relax[:, side]
        share = rate / (1.0 + rate)
        moments = mom_out[stage]
        for p in range(1, count):
            mom_copy(stage, p).wait_recv()
            moments += mom_in[stage, p - 1]
        coeffs = [
            share * sum(inverse[k][l] * moments[l : l + 1, :] for l in range(5)) for k in range(5)
        ]
        keep = 1.0 - share
        last = stage + HALVES >= STEPS * HALVES
        if last:
            constant_ref[:, side] = coeffs[0]
        for base in range(0, rows, PART):
            vx, vy, vz = row_speeds(first_node + base, PART)
            squares = vx * vx + vy * vy + vz * vz
            part = keep * acc[pl.ds(base, PART), side]
            part += vx * coeffs[1] + vy * coeffs[2] + vz * coeffs[3] + squares * coeffs[4]
            if last:
                out_ref[pl.ds(HALVES * base + half, PART, stride=HALVES), :] = part
            else:
                part += coeffs[0]
                state[pl.ds(base, PART), side] = part
                publish_block(stage + HALVES, base, part)
        if not last:
            send_own(stage + HALVES)
            for base in range(0, rows, PART):
                publish_planes(stage + HALVES, base, state[pl.ds(base, PART), side])
            send_planes(stage + HALVES)

    relay(0)
    send_own(1, own[len(own) // 2 :])
    advect(0)
    kernel_term(0)
    send_moments(0)
    relay(1)
    inverse = invert()
    relax_half(0, inverse)
    kernel_term(1)
    send_moments(1)
    relay(2)
    relax_half(1, inverse)
    kernel_term(2, fresh=True)
    relay(3)
    advect(1)
    send_moments(2)
    kernel_term(3)
    send_moments(3)
    relax_half(2, inverse)
    relax_half(3, inverse)

    for copy in pending:
        copy.wait_send()


def per_device(count, slabs, distribution, relax_rate, node_weight, kernel_tiles, tile_cols):
    rows, depth, cells = distribution.shape
    assert depth == 1 and cells == 256 and rows % CHUNK == 0
    row_blocks, listed = tile_cols.shape
    chunks = rows // CHUNK
    slots = jnp.arange(listed, dtype=jnp.int32)[None, :, None]
    match = tile_cols[:, :, None] == jnp.arange(RBLK, dtype=jnp.int32)[None, None, :]
    places = listed + jnp.sum(jnp.where(match, slots - listed, 0), axis=1)
    keys = 3 * chunks if count == 4 else (count - 1) * chunks
    peers = count - 1
    stages = STEPS * HALVES
    lanes = cells // HALVES
    vmem = pl.BlockSpec(memory_space=pltpu.VMEM)
    dma = pltpu.SemaphoreType.DMA
    result, constant = pl.pallas_call(
        functools.partial(kernel, count, slabs),
        out_shape=(
            jax.ShapeDtypeStruct((rows * HALVES, lanes), F32),
            jax.ShapeDtypeStruct((1, cells), F32),
        ),
        in_specs=[pl.BlockSpec(memory_space=pltpu.SMEM)] + [pl.BlockSpec(memory_space=pltpu.HBM)] * 4,
        out_specs=(vmem, vmem),
        scratch_shapes=[
            pltpu.VMEM((listed + 1, row_blocks, TILE, TILE), BF16),
            pltpu.VMEM((V // CHUNK, rows, CHUNK), BF16),
            pltpu.VMEM((rows * HALVES, lanes), F32),
            pltpu.VMEM((1, cells), F32),
            pltpu.VMEM((1, rows), F32),
            pltpu.VMEM((rows, cells), F32),
            pltpu.VMEM((rows, cells), F32),
            pltpu.VMEM((stages, V // CHUNK, CHUNK, lanes), BF16),
            pltpu.VMEM((stages, 2, rows // 2, lanes), BF16),
            pltpu.VMEM((stages, 2, rows // 2, lanes), BF16),
            pltpu.VMEM((stages, 8, lanes), F32),
            pltpu.VMEM((stages, peers, 8, lanes), F32),
            pltpu.VMEM((5, 8, lanes), F32),
            pltpu.VMEM((peers, 5, 8, lanes), F32),
            pltpu.VMEM((16, rows), BF16),
            dma((listed,)),
            dma((chunks,)),
            dma((2,)),
            dma((stages, keys)),
            dma((stages, keys)),
            dma((stages, 2)),
            dma((stages, 2)),
            dma((stages, peers)),
            dma((stages, peers)),
            dma((peers,)),
            dma((peers,)),
        ],
        compiler_params=pltpu.CompilerParams(
            collective_id=0, has_side_effects=True, vmem_limit_bytes=63 * 1024 * 1024
        ),
        name="bgk_steps",
    )(
        places, kernel_tiles, distribution.reshape(rows * HALVES, lanes), relax_rate,
        node_weight.reshape(1, rows),
    )
    return result.reshape(rows, depth, cells) + constant[None]


def solution(mesh):
    placed = (
        P("vert", "gx", None),
        P("gx", None),
        P("vert"),
        P("vert", None, None),
        P("vert", None),
    )
    return jax.shard_map(
        functools.partial(per_device, mesh.shape["vert"], mesh.shape["gx"]),
        mesh=mesh, in_specs=placed, out_specs=P("vert", "gx", None), check_vma=False,
    )
```

```python
import functools

import jax
import jax.numpy as jnp
from jax import lax
from jax.experimental import pallas as pl
from jax.experimental.pallas import tpu as pltpu
from jax.sharding import PartitionSpec as P

Q = 16
TILE = 128
NZ = 4
STEPS = 2
HALVES = 2
V = 4096
RBLK = 32
CHUNK = 256
PART = 128
COURANT_SCALE = 0.3
KERNEL_STEP = 0.5
MESH = pl.DeviceIdType.MESH
F32 = jnp.float32
BF16 = jnp.bfloat16


def speeds(node_index):
    middle = (Q - 1) / 2.0
    speed_x = ((node_index & (Q - 1)).astype(F32) - middle) / middle
    speed_y = ((lax.shift_right_logical(node_index, 4) & (Q - 1)).astype(F32) - middle) / middle
    speed_z = (lax.shift_right_logical(node_index, 8).astype(F32) - middle) / middle
    return speed_x, speed_y, speed_z


def row_speeds(first, rows):
    return speeds(first + lax.broadcasted_iota(jnp.int32, (rows, 1), 0))


def vert_plan(me, count, chunks):
    if count == 4:
        x, y = lax.rem(me, 2), lax.div(me, 2)
        px, py, pd = y * 2 + (1 - x), (1 - y) * 2 + x, 3 - me
        half = chunks // 2
        first = list(range(half))
        second = list(range(half, chunks))
        to_x = [(c, px, me, c) for c in first + second]
        to_y = [(chunks + c, py, me, c) for c in second + first]
        own = [send for pair in zip(to_x, to_y) for send in pair]
        from_x = [(c, px, c) for c in first + second]
        from_y = [(chunks + c, py, c) for c in second + first]
        arrivals = [item for pair in zip(from_x, from_y) for item in pair]
        forwards = {}
        for c in first:
            forwards[c] = (2 * chunks + c, py, px, c)
        for c in second:
            forwards[chunks + c] = (2 * chunks + c, px, py, c)
        late = [c for pair in zip(first, second) for c in pair]
        arrivals += [(2 * chunks + c, pd, c) for c in late]
        return own, arrivals, forwards
    own, arrivals = [], []
    for p in range(1, count):
        for c in range(chunks):
            key = (p - 1) * chunks + c
            own.append((key, lax.rem(me + p, count), me, c))
            arrivals.append((key, lax.rem(me + count - p, count), c))
    return own, arrivals, {}


def kernel(
    count, slabs, place_ref, tiles_ref, dist_ref, relax_ref, weight_ref, out_ref, constant_ref,
    tiles, dense, source_rows, relax, node_weight, state, acc, gathered, plane_out, plane_in,
    mom_out, mom_in, gram_out, gram_in, weights2, tile_sem, source_sem, small_sem, vert_send,
    vert_recv, plane_send, plane_recv, mom_send, mom_recv, gram_send, gram_recv,
):
    rows, cells = state.shape
    lanes = cells // HALVES
    chunks = rows // CHUNK
    row_blocks = rows // TILE
    listed = tiles_ref.shape[2] // TILE
    me = lax.axis_index("vert")
    slab = lax.axis_index("gx")
    above = lax.rem(slab + 1, slabs)
    below = lax.rem(slab + slabs - 1, slabs)
    first_node = me * rows

    barrier = pltpu.get_barrier_semaphore()
    for p in range(1, count):
        pl.semaphore_signal(
            barrier, inc=1, device_id=(slab, lax.rem(me + p, count)), device_id_type=MESH
        )
    for other in (below, above):
        pl.semaphore_signal(barrier, inc=1, device_id=(other, me), device_id_type=MESH)

    source_loads = []
    for c in range(chunks):
        span = pl.ds(HALVES * CHUNK * c, HALVES * CHUNK)
        source_loads.append(
            pltpu.make_async_copy(dist_ref.at[span, :], source_rows.at[span, :], source_sem.at[c])
        )
    small_loads = [
        pltpu.make_async_copy(weight_ref, node_weight, small_sem.at[0]),
        pltpu.make_async_copy(relax_ref, relax, small_sem.at[1]),
    ]
    loads = [
        pltpu.make_async_copy(
            tiles_ref.at[:, :, pl.ds(j * TILE, TILE)], tiles.at[j], tile_sem.at[j]
        )
        for j in range(listed)
    ]
    for load in source_loads + small_loads + loads:
        load.start()

    own, arrivals, forwards = vert_plan(me, count, chunks)
    early = [item for item in arrivals if item[0] in forwards]
    rest = [item for item in arrivals if item[0] not in forwards]
    pending = []

    def vert_copy(stage, key, target, block, chunk):
        where = gathered.at[stage, block * chunks + chunk]
        return pltpu.make_async_remote_copy(
            src_ref=where, dst_ref=where, send_sem=vert_send.at[stage, key],
            recv_sem=vert_recv.at[stage, key], device_id=(slab, target), device_id_type=MESH,
        )

    def plane_copy(stage, side):
        return pltpu.make_async_remote_copy(
            src_ref=plane_out.at[stage, side], dst_ref=plane_in.at[stage, side],
            send_sem=plane_send.at[stage, side], recv_sem=plane_recv.at[stage, side],
            device_id=(above if side == 1 else below, me), device_id_type=MESH,
        )

    def mom_copy(stage, p):
        return pltpu.make_async_remote_copy(
            src_ref=mom_out.at[stage], dst_ref=mom_in.at[stage, p - 1],
            send_sem=mom_send.at[stage, p - 1], recv_sem=mom_recv.at[stage, p - 1],
            device_id=(slab, lax.rem(me + p, count)), device_id_type=MESH,
        )

    def gram_copy(p):
        return pltpu.make_async_remote_copy(
            src_ref=gram_out, dst_ref=gram_in.at[p - 1],
            send_sem=gram_send.at[p - 1], recv_sem=gram_recv.at[p - 1],
            device_id=(slab, lax.rem(me + p, count)), device_id_type=MESH,
        )

    def start(copy):
        copy.start()
        pending.append(copy)

    def publish_block(stage, base, part):
        chunk, inner = base // CHUNK, base % CHUNK
        gathered[stage, me * chunks + chunk, pl.ds(inner, PART), :] = part.astype(BF16)

    def publish_planes(stage, base, part):
        groups = part.reshape(PART // Q, 2, Q // 2, lanes)
        for side in range(2):
            plane_out[stage, side, pl.ds(base // 2, PART // 2), :] = (
                groups[:, side].reshape(PART // 2, lanes).astype(BF16)
            )

    def send_own(stage, items=own):
        for item in items:
            start(vert_copy(stage, *item))

    def send_planes(stage):
        for side in range(2):
            start(plane_copy(stage, side))

    for half in range(HALVES):
        for base in range(0, rows, PART):
            if half == 0 and base % CHUNK == 0:
                source_loads[base // CHUNK].wait()
            part = source_rows[pl.ds(HALVES * base + half, PART, stride=HALVES), :]
            state[pl.ds(base, PART), pl.ds(half * lanes, lanes)] = part
            publish_block(half, base, part)
        if half == 0:
            pl.semaphore_wait(barrier, count + 1)
            send_own(0)
        else:
            send_own(1, own[: len(own) // 2])
    for half in range(HALVES):
        for base in range(0, rows, PART):
            publish_planes(half, base, state[pl.ds(base, PART), pl.ds(half * lanes, lanes)])
        send_planes(half)

    for load in small_loads:
        load.wait()
    lane_node = first_node + lax.broadcasted_iota(jnp.int32, (8, rows), 1)
    kind = lax.broadcasted_iota(jnp.int32, (8, rows), 0)
    sx, sy, sz = speeds(lane_node)
    kinds = [jnp.ones_like(sx), sx, sy, sz, sx * sx + sy * sy + sz * sz]
    invariants = jnp.zeros_like(sx)
    for k, row in enumerate(kinds):
        invariants = jnp.where(kind == k, row, invariants)
    weighted = invariants * node_weight[...]
    high = weighted.astype(BF16).astype(F32)
    weights2[...] = jnp.concatenate([high, weighted - high], axis=0).astype(BF16)
    for l in range(5):
        column = jnp.sum(weighted * kinds[l], axis=1, keepdims=True)
        gram_out[l] = jnp.broadcast_to(column, (8, lanes))
    for p in range(1, count):
        start(gram_copy(p))

    tiles[listed] = jnp.zeros((row_blocks, TILE, TILE), BF16)
    for load in loads:
        load.wait()
    per_chunk = CHUNK // TILE

    def expand(index, carry):
        k, r = lax.div(index, row_blocks), lax.rem(index, row_blocks)
        here = pl.ds(pl.multiple_of(r * TILE, TILE), TILE)
        for b in range(per_chunk):
            place = place_ref[r, k * per_chunk + b]
            dense[k, here, pl.ds(b * TILE, TILE)] = tiles[place, r]
        return carry

    lax.fori_loop(0, (V // CHUNK) * row_blocks, expand, 0, unroll=4)

    def advect(step):
        for half in range(HALVES):
            for side in range(2):
                plane_copy(step * HALVES + half, side).wait_recv()

        def one(i, carry):
            base = pl.multiple_of(i * PART, PART)
            source = state[pl.ds(base, PART), :]
            planes = pl.ds(pl.multiple_of(i * (PART // 2), PART // 2), PART // 2)
            sides = [
                jnp.concatenate(
                    [plane_in[step * HALVES + half, side, planes, :] for half in range(HALVES)],
                    axis=1,
                ).astype(F32).reshape(PART // Q, 1, Q // 2, cells)
                for side in range(2)
            ]
            upwind_x = jnp.concatenate(sides, axis=1).reshape(PART, cells)
            px, py, pz = [COURANT_SCALE * s for s in row_speeds(first_node + base, PART)]
            z_index = lax.broadcasted_iota(jnp.int32, (PART, cells), 1) & (NZ - 1)
            lower_y = pltpu.roll(source, NZ, 1)
            upper_y = pltpu.roll(source, cells - NZ, 1)
            lower_z = jnp.where(
                z_index == 0, pltpu.roll(source, cells + 1 - NZ, 1), pltpu.roll(source, 1, 1)
            )
            upper_z = jnp.where(
                z_index == NZ - 1, pltpu.roll(source, NZ - 1, 1), pltpu.roll(source, cells - 1, 1)
            )
            flux = jnp.abs(px) * (source - upwind_x)
            flux += jnp.maximum(py, 0.0) * (source - lower_y) + jnp.minimum(py, 0.0) * (
                upper_y - source
            )
            flux += jnp.maximum(pz, 0.0) * (source - lower_z) + jnp.minimum(pz, 0.0) * (
                upper_z - source
            )
            result = source - flux
            if step == 0:
                acc[pl.ds(base, PART), :] = result
            else:
                acc[pl.ds(base, PART), pl.ds(0, lanes)] += result[:, :lanes]
                acc[pl.ds(base, PART), pl.ds(lanes, cells - lanes)] = result[:, lanes:]
            return carry

        lax.fori_loop(0, rows // PART, one, 0)

    def multiply(stage, indices, fresh=False):
        side = pl.ds(stage % HALVES * lanes, lanes)

        def one(i, carry):
            here = pl.ds(pl.multiple_of(i * CHUNK, CHUNK), CHUNK)
            total = jnp.zeros((CHUNK, lanes), F32)
            for index in indices:
                total += jnp.dot(
                    dense[index, here, :], gathered[stage, index], preferred_element_type=F32
                )
            if fresh:
                acc[here, side] = KERNEL_STEP * total
            else:
                acc[here, side] += KERNEL_STEP * total
            return carry

        lax.fori_loop(0, rows // CHUNK, one, 0, unroll=True)

    def arrive(stage, item):
        key, block, chunk = item
        vert_copy(stage, key, me, block, chunk).wait_recv()
        if key in forwards:
            start(vert_copy(stage, *forwards[key]))

    def relay(stage):
        for item in early:
            arrive(stage, item)

    def kernel_term(stage, fresh=False):
        ready = [me * chunks + chunk for chunk in range(chunks)]
        multiply(stage, ready + [block * chunks + chunk for _, block, chunk in early], fresh)
        for at in range(0, len(rest), 2):
            for item in rest[at : at + 2]:
                arrive(stage, item)
            multiply(stage, [block * chunks + chunk for _, block, chunk in rest[at : at + 2]])

    def send_moments(stage):
        side = pl.ds(stage % HALVES * lanes, lanes)
        total = jnp.zeros((16, lanes), F32)
        for base in range(0, rows, CHUNK):
            explicit = acc[pl.ds(base, CHUNK), side]
            top = explicit.astype(BF16)
            low = (explicit - top.astype(F32)).astype(BF16)
            left = weights2[:, pl.ds(base, CHUNK)]
            total += jnp.dot(left, top, preferred_element_type=F32)
            total += jnp.dot(left, low, preferred_element_type=F32)
        mom_out[stage] = total[:8] + total[8:]
        for p in range(1, count):
            start(mom_copy(stage, p))

    def invert():
        gram = gram_out[...]
        for p in range(1, count):
            gram_copy(p).wait_recv()
            gram += gram_in[p - 1]
        matrix = [[gram[l, k : k + 1, :] for l in range(5)] for k in range(5)]
        one, none = jnp.ones((1, lanes), F32), jnp.zeros((1, lanes), F32)
        inverse = [[one if k == l else none for l in range(5)] for k in range(5)]
        for k in range(5):
            scale = 1.0 / matrix[k][k]
            matrix[k] = [entry * scale for entry in matrix[k]]
            inverse[k] = [entry * scale for entry in inverse[k]]
            for r in range(5):
                if r != k:
                    factor = matrix[r][k]
                    matrix[r] = [a - factor * b for a, b in zip(matrix[r], matrix[k])]
                    inverse[r] = [a - factor * b for a, b in zip(inverse[r], inverse[k])]
        return inverse

    def relax_half(stage, inverse):
        half = stage % HALVES
        side = pl.ds(half * lanes, lanes)
        rate = relax[:, side]
        share = rate / (1.0 + rate)
        moments = mom_out[stage]
        for p in range(1, count):
            mom_copy(stage, p).wait_recv()
            moments += mom_in[stage, p - 1]
        coeffs = [
            share * sum(inverse[k][l] * moments[l : l + 1, :] for l in range(5)) for k in range(5)
        ]
        keep = 1.0 - share
        last = stage + HALVES >= STEPS * HALVES
        if last:
            constant_ref[:, side] = coeffs[0]
        for base in range(0, rows, PART):
            vx, vy, vz = row_speeds(first_node + base, PART)
            squares = vx * vx + vy * vy + vz * vz
            part = keep * acc[pl.ds(base, PART), side]
            part += vx * coeffs[1] + vy * coeffs[2] + vz * coeffs[3] + squares * coeffs[4]
            if last:
                out_ref[pl.ds(HALVES * base + half, PART, stride=HALVES), :] = part
            else:
                part += coeffs[0]
                state[pl.ds(base, PART), side] = part
                publish_block(stage + HALVES, base, part)
        if not last:
            send_own(stage + HALVES)
            for base in range(0, rows, PART):
                publish_planes(stage + HALVES, base, state[pl.ds(base, PART), side])
            send_planes(stage + HALVES)

    relay(0)
    send_own(1, own[len(own) // 2 :])
    advect(0)
    inverse = invert()
    kernel_term(0)
    send_moments(0)
    relay(1)
    relax_half(0, inverse)
    kernel_term(1)
    send_moments(1)
    relay(2)
    relax_half(1, inverse)
    kernel_term(2, fresh=True)
    relay(3)
    advect(1)
    send_moments(2)
    kernel_term(3)
    send_moments(3)
    relax_half(2, inverse)
    relax_half(3, inverse)

    for copy in pending:
        copy.wait_send()


def per_device(count, slabs, distribution, relax_rate, node_weight, kernel_tiles, tile_cols):
    rows, depth, cells = distribution.shape
    assert depth == 1 and cells == 256 and rows % CHUNK == 0
    row_blocks, listed = tile_cols.shape
    chunks = rows // CHUNK
    slots = jnp.arange(listed, dtype=jnp.int32)[None, :, None]
    match = tile_cols[:, :, None] == jnp.arange(RBLK, dtype=jnp.int32)[None, None, :]
    places = listed + jnp.sum(jnp.where(match, slots - listed, 0), axis=1)
    keys = 3 * chunks if count == 4 else (count - 1) * chunks
    peers = count - 1
    stages = STEPS * HALVES
    lanes = cells // HALVES
    vmem = pl.BlockSpec(memory_space=pltpu.VMEM)
    dma = pltpu.SemaphoreType.DMA
    result, constant = pl.pallas_call(
        functools.partial(kernel, count, slabs),
        out_shape=(
            jax.ShapeDtypeStruct((rows * HALVES, lanes), F32),
            jax.ShapeDtypeStruct((1, cells), F32),
        ),
        in_specs=[pl.BlockSpec(memory_space=pltpu.SMEM)] + [pl.BlockSpec(memory_space=pltpu.HBM)] * 4,
        out_specs=(vmem, vmem),
        scratch_shapes=[
            pltpu.VMEM((listed + 1, row_blocks, TILE, TILE), BF16),
            pltpu.VMEM((V // CHUNK, rows, CHUNK), BF16),
            pltpu.VMEM((rows * HALVES, lanes), F32),
            pltpu.VMEM((1, cells), F32),
            pltpu.VMEM((1, rows), F32),
            pltpu.VMEM((rows, cells), F32),
            pltpu.VMEM((rows, cells), F32),
            pltpu.VMEM((stages, V // CHUNK, CHUNK, lanes), BF16),
            pltpu.VMEM((stages, 2, rows // 2, lanes), BF16),
            pltpu.VMEM((stages, 2, rows // 2, lanes), BF16),
            pltpu.VMEM((stages, 8, lanes), F32),
            pltpu.VMEM((stages, peers, 8, lanes), F32),
            pltpu.VMEM((5, 8, lanes), F32),
            pltpu.VMEM((peers, 5, 8, lanes), F32),
            pltpu.VMEM((16, rows), BF16),
            dma((listed,)),
            dma((chunks,)),
            dma((2,)),
            dma((stages, keys)),
            dma((stages, keys)),
            dma((stages, 2)),
            dma((stages, 2)),
            dma((stages, peers)),
            dma((stages, peers)),
            dma((peers,)),
            dma((peers,)),
        ],
        compiler_params=pltpu.CompilerParams(
            collective_id=0, has_side_effects=True, vmem_limit_bytes=63 * 1024 * 1024
        ),
        name="bgk_steps",
    )(
        places, kernel_tiles, distribution.reshape(rows * HALVES, lanes), relax_rate,
        node_weight.reshape(1, rows),
    )
    return result.reshape(rows, depth, cells) + constant[None]


def solution(mesh):
    placed = (
        P("vert", "gx", None),
        P("gx", None),
        P("vert"),
        P("vert", None, None),
        P("vert", None),
    )
    return jax.shard_map(
        functools.partial(per_device, mesh.shape["vert"], mesh.shape["gx"]),
        mesh=mesh, in_specs=placed, out_specs=P("vert", "gx", None), check_vma=False,
    )
```
